32 devices in a mesh: inline: 4 (over z), xline: 8 (over y, x, core).
Axes of the slice: x: 2, y: 2, z: 4, core: 2. Of those that a mesh axis runs over, the one named last changes fastest.
Arguments:
- right_side: float32 [32, 256, 128], P('inline', 'xline'), may hold values from -9 to 9, as said below
- facies: int32 [32, 256, 128], P('inline', 'xline'), may hold values from 0 to 7
- facies_table: float32 [2, 8], replicated, may hold values from 0.2 to 5
- thickness: float32 [32, 256, 128], P('inline', 'xline'), may hold values from 0.5 to 2
- accumulation: float32 [32, 256, 128], P('inline', 'xline'), may hold values from 0.2 to 2
- perforation_cell: int32 [131072], P(('inline', 'xline')), may hold values from 0 to 32767
- perf_owner: int32 [131072, 1], P(('inline', 'xline')), may hold values from 0 to 31; in each aligned block of 4096 rows (0 to 4095, 4096 to 8191, ...) at most 512 rows name the same one
- perf_well: int32 [131072], P(('inline', 'xline')), may hold values from 0 to 159
- perf_index: float32 [131072], P(('inline', 'xline')), may hold values from 0.5 to 5
Outputs:
- pressure: float32 [32, 256, 128], P('inline', 'xline')
- residual: float32 [32, 256, 128], P('inline', 'xline')
The draws below stay inside these ranges and needn't reach their ends.
Inputs may be any that keep to these rules, and one draw needn't show every extreme that they name: `perforation_cell`: local flat index of a cell of the device that holds the row. `perf_owner`: device index over inline+xline; among the rows of one device at most 512 name the same owner, and that bound is reached. `right_side`: rough values of either sign.
All inputs are finite; a program needn't handle non-finite values.
Results may differ from the reference program's by a relative error of at most 0.0001.
Values sent between devices are 32-bit elements; how exact they have to be, the bound alone decides.
No kernel may reach another device: no remote copies, remote signals or barrier semaphores. Data moves between devices by JAX's collectives and lax.ppermute only.
A program may use at most 64 MiB of HBM per device.

```python
import math
import jax
import jax.numpy as jnp
import numpy as np

CI = 8
CX = 32
NZ = 128
NF = 8
SWEEPS = 3
PERF_DEV = 4096
WELL_DEV = 160
CAP = 512
NI = 32
NXL = 256
N_INLINE = 4
N_XLINE = 8
DEVICES = 32


def draw_right_side(key, part):
    shape = (NI, NXL, NZ)
    return jnp.clip(3.0 * jax.random.normal(key, shape, jnp.float32), -9.0, 9.0)


def plant(drawn, own_key, least, largest):
    place = [jax.random.randint(jax.random.fold_in(own_key, axis), (), 0, length) for axis, length in enumerate(drawn.shape)]
    main_axis = drawn.shape.index(max(drawn.shape))
    neighbour = place[:main_axis] + [(place[main_axis] + 1) % drawn.shape[main_axis]] + place[main_axis + 1:]
    return drawn.at[tuple(place)].set(least).at[tuple(neighbour)].set(largest)


def shard_levels(rng, shape, cuts, low, largest):
    loudness = 1.0
    for dim, shards_of in cuts:
        draws = jax.random.uniform(jax.random.fold_in(jax.random.fold_in(rng, 6), dim), (shards_of,), jnp.float32, low / len(cuts), largest / len(cuts))
        loudness = loudness * jnp.repeat(jnp.exp(draws), shape[dim] // shards_of).reshape((-1,) + (1,) * (len(shape) - 1 - dim))
    return loudness


def routed_block(stream_key, own, number, rows, count, top, most, slope):
    sequence = jax.random.permutation(stream_key, count)
    heavy_load, common = load_shares(count, rows * top, most, slope, True), load_shares(count, rows * top, most, slope, False)
    places = jnp.arange(count)

    def named(sizes, offset_by):
        used = int((sizes > 0).sum())
        fixed = max(1, used // 4)
        passed = fixed + (places - fixed + offset_by * (used - fixed)) % max(1, count - fixed)
        return jnp.zeros((count,), jnp.int32).at[sequence[jnp.where(places < fixed, places, passed)]].set(jnp.asarray(sizes, jnp.int32))

    sizes = jnp.where(number % 4 == 0, named(heavy_load, number // 4), named(common, number - number // 4 - 1))
    mixed = jax.random.permutation(jax.random.fold_in(own, 3), count)
    donor, receiver = mixed[0:count // 2 * 2:2], mixed[1:count // 2 * 2:2]
    slack = jnp.minimum(sizes[donor] - 1, most - sizes[receiver]) // 2
    slack = jnp.where((donor == sequence[0]) | (receiver == sequence[0]) | (sizes[receiver] == 0), 0, jnp.maximum(slack, 0))
    passed = jax.random.randint(jax.random.fold_in(own, 4), (count // 2,), 0, 1 << 20) % (slack + 1)
    sizes = sizes.at[donor].add(-passed).at[receiver].add(passed)
    labels = jnp.searchsorted(jnp.cumsum(sizes), jnp.arange(rows * top), side="right").astype(jnp.int32)
    table = labels.reshape(top, rows).T
    table = table[jax.random.permutation(jax.random.fold_in(own, 1), rows)]
    offset_by = jax.random.randint(jax.random.fold_in(own, 2), (rows, 1), 0, top)
    return jnp.take_along_axis(table, (jnp.arange(top)[None, :] + offset_by) % top, axis=1)


def load_shares(amount, total, most, lean, full):
    portions = [(1 << 20) // math.isqrt(grade ** lean) + 1 for grade in range(1, amount + 1)]
    largest = most if full else min(most, max(-(-total // amount), total * portions[0] // sum(portions)))
    least = 1 if total - largest >= amount - 1 else 0
    given, spare = [largest] + [least] * (amount - 1), total - largest - least * (amount - 1)
    while spare > 0:
        free = [i for i in range(1, amount) if given[i] < largest] or [i for i in range(1, amount) if given[i] < most]
        pool, left = sum([portions[i] for i in free]), spare
        for i in free:
            extra = min(most - given[i], max(1, left * portions[i] // pool), spare)
            given[i] = given[i] + extra
            spare = spare - extra
    return np.array(given)


def setup_inputs(seed: int = 0) -> dict:
    key_of = jax.random.split(jax.random.key(seed), 10)
    right_side = draw_right_side(jax.random.fold_in(key_of[9], 71), 0)
    facies = plant(jax.random.randint(key_of[1], (NI, NXL, NZ), 0, NF), jax.random.fold_in(key_of[1], 1), 0, NF - 1).astype(jnp.int32)
    facies_table = jnp.clip(jnp.exp(jax.random.uniform(key_of[2], (2, NF), jnp.float32, math.log(0.2), math.log(5.0))), 0.2, 5.0)
    thickness = jnp.clip(jnp.exp(math.log(2.0) - 1.3862944 * jax.random.uniform(key_of[3], (NI, NXL, NZ), jnp.float32) ** shard_levels(key_of[3], (NI, NXL, NZ), ((0, 4), (1, 8)), -0.2, 0.2)), 0.5, 2.0)
    accumulation = jnp.clip(jnp.exp(math.log(2.0) - 2.3025851 * jax.random.uniform(key_of[4], (NI, NXL, NZ), jnp.float32) ** shard_levels(key_of[4], (NI, NXL, NZ), ((0, 4), (1, 8)), -0.2, 0.2)), 0.2, 2.0)
    perforation_cell = plant(jax.random.randint(key_of[5], (DEVICES * PERF_DEV,), 0, CI * CX * NZ), jax.random.fold_in(key_of[5], 1), 0, (CI * CX * NZ) - 1).astype(jnp.int32)
    perf_owner_keys = jax.random.split(jax.random.fold_in(key_of[6], 1), (DEVICES * PERF_DEV) // PERF_DEV)
    perf_owner_turns = jax.random.permutation(jax.random.fold_in(key_of[6], 3), (DEVICES * PERF_DEV) // PERF_DEV)
    perf_owner = jax.vmap(lambda own, number: routed_block(jax.random.fold_in(key_of[6], 2), own, number, PERF_DEV, DEVICES, 1, CAP, 2))(perf_owner_keys, perf_owner_turns).reshape((DEVICES * PERF_DEV, 1))
    perf_well = plant(jax.random.randint(key_of[7], (DEVICES * PERF_DEV,), 0, WELL_DEV), jax.random.fold_in(key_of[7], 1), 0, WELL_DEV - 1).astype(jnp.int32)
    perf_index = jnp.clip(jnp.exp(math.log(5.0) - 2.3025851 * jax.random.uniform(key_of[8], (DEVICES * PERF_DEV,), jnp.float32) ** shard_levels(key_of[8], (DEVICES * PERF_DEV,), ((0, 32),), -0.2, 0.2)), 0.5, 5.0)
    return {"right_side": right_side, "facies": facies, "facies_table": facies_table, "thickness": thickness, "accumulation": accumulation, "perforation_cell": perforation_cell, "perf_owner": perf_owner, "perf_well": perf_well, "perf_index": perf_index}


LOW_BOUND = 0.1
HIGH_BOUND = 2.0


def harmonic_average(first, second):
    return 2.0 * first * second / (first + second)


def reference(right_side, facies, facies_table, thickness, accumulation, perforation_cell, perf_owner, perf_well, perf_index):
    lateral = facies_table[0][facies] * thickness
    vertical_trans = facies_table[1][facies] / thickness
    padded = jnp.pad(lateral, ((1, 1), (1, 1), (0, 0)))
    inline_lower_face = harmonic_average(lateral, padded[:-2, 1:-1])
    face_iplus = harmonic_average(lateral, padded[2:, 1:-1])
    face_jmin = harmonic_average(lateral, padded[1:-1, :-2])
    face_jplus = harmonic_average(lateral, padded[1:-1, 2:])
    vertical_padding = jnp.pad(vertical_trans, ((0, 0), (0, 0), (1, 1)))
    depth_lower_face = harmonic_average(vertical_trans, vertical_padding[:, :, :-2])
    depth_upper_face = harmonic_average(vertical_trans, vertical_padding[:, :, 2:])
    devices = N_INLINE * N_XLINE
    rows = jnp.arange(devices * PERF_DEV, dtype=jnp.int32)
    device = rows // PERF_DEV
    dev_in = device // N_XLINE
    dev_x = device % N_XLINE
    cell_i = perforation_cell // (CX * NZ)
    cell_x = (perforation_cell // NZ) % CX
    cell_z = perforation_cell % NZ
    flat = ((dev_in * CI + cell_i) * NXL + dev_x * CX + cell_x) * NZ + cell_z
    flat = flat.astype(jnp.int32)
    ncell = NI * NXL * NZ
    nwell = WELL_DEV * devices
    well_id = (perf_owner[:, 0] * WELL_DEV + perf_well).astype(jnp.int32)
    storage = 1.0 + jax.ops.segment_sum(perf_index, well_id, num_segments=nwell)
    cell_wi = jax.ops.segment_sum(perf_index, flat, num_segments=ncell).reshape(right_side.shape)
    diagonal = accumulation + inline_lower_face + face_iplus + face_jmin + face_jplus + depth_lower_face + depth_upper_face + cell_wi

    def operate(field):
        beside_all = jnp.pad(field, ((1, 1), (1, 1), (0, 0)))
        zpad = jnp.pad(field, ((0, 0), (0, 0), (1, 1)))
        grid = accumulation * field
        grid = grid + inline_lower_face * (field - beside_all[:-2, 1:-1]) + face_iplus * (field - beside_all[2:, 1:-1])
        grid = grid + face_jmin * (field - beside_all[1:-1, :-2]) + face_jplus * (field - beside_all[1:-1, 2:])
        grid = grid + depth_lower_face * (field - zpad[:, :, :-2]) + depth_upper_face * (field - zpad[:, :, 2:])
        local = field.reshape(-1)[flat]
        bottom = jax.ops.segment_sum(perf_index * local, well_id, num_segments=nwell) / storage
        terms = perf_index * (local - bottom[well_id])
        wells = jax.ops.segment_sum(terms, flat, num_segments=ncell).reshape(field.shape)
        return grid + wells

    theta = (HIGH_BOUND + LOW_BOUND) / 2.0
    delta = (HIGH_BOUND - LOW_BOUND) / 2.0
    sigma = theta / delta
    rho_now = 1.0 / sigma
    pressure = jnp.zeros_like(right_side)
    residual = right_side
    direction = residual / (theta * diagonal)
    for sweep in range(SWEEPS):
        pressure = pressure + direction
        residual = residual - operate(direction)
        if sweep + 1 < SWEEPS:
            rho_next = 1.0 / (2.0 * sigma - rho_now)
            direction = (rho_next * rho_now) * direction + (2.0 * rho_next / delta) * (residual / diagonal)
            rho_now = rho_next
    return pressure, residual
```

```python
import functools

import jax
import jax.numpy as jnp
from jax import lax
from jax.experimental import pallas as pl
from jax.experimental.pallas import tpu as pltpu
from jax.sharding import PartitionSpec as P

SWEEPS = 3
WELL_DEV = 160
LANES = 128
LOW_BOUND = 0.1
HIGH_BOUND = 2.0
CHUNK = 512
MESH_AXES = ("inline", "xline")

VMEM = pl.BlockSpec(memory_space=pltpu.VMEM)
SMEM = pl.BlockSpec(memory_space=pltpu.SMEM)
PARAMS = pltpu.CompilerParams(vmem_limit_bytes=40 * 1024 * 1024)


def xor_permute(value, axis, mask):
    count = lax.axis_size(axis)
    return lax.ppermute(value, axis, [(i, i ^ mask) for i in range(count)])


def bits_of(count):
    bits = count.bit_length() - 1
    if 1 << bits != count:
        raise ValueError("axis size")
    return bits


def side_masks(count):
    return [(2 << s) - 1 for s in range(bits_of(count))]


def stages_of(count):
    bits = bits_of(count)
    cuts = ([1] if bits % 2 else []) + [2] * (bits // 2)
    stages, low = [], 0
    for width in cuts:
        masks = []
        for pattern in range(1, 1 << width):
            mask = pattern << low
            if pattern & (pattern + 1) == 0:
                mask |= (1 << low) - 1
            masks.append(mask)
        stages.append(masks)
        low += width
    return stages


def all_sum(value, sides):
    arrived = {}
    rows = value.shape[0]
    for axis in ("xline", "inline"):
        count = lax.axis_size(axis)
        carried = side_masks(count)
        for masks in stages_of(count):
            total = value
            for mask in masks:
                if mask in carried:
                    face = sides[axis][0 if mask == 1 else 1]
                    got = xor_permute(jnp.concatenate([value, face], axis=0), axis, mask)
                    arrived[axis, mask] = got[rows:]
                    total = total + got[:rows]
                else:
                    total = total + xor_permute(value, axis, mask)
            value = total
    return value, halos(arrived)


def side_exchange(sides):
    arrived = {}
    for axis in ("inline", "xline"):
        for mask in side_masks(lax.axis_size(axis)):
            arrived[axis, mask] = xor_permute(sides[axis][0 if mask == 1 else 1], axis, mask)
    return halos(arrived)


def halos(arrived):
    result = {}
    for axis in MESH_AXES:
        index = lax.axis_index(axis)
        even = index % 2 == 0
        other = jnp.where(even, index - 1, index + 1)
        beside = arrived[axis, 1]
        far = beside
        for mask in side_masks(lax.axis_size(axis))[1:]:
            far = jnp.where((index ^ other) == mask, arrived[axis, mask], far)
        result[axis] = (jnp.where(even, far, beside), jnp.where(even, beside, far))
    return result


def sides_of(lower, upper, axis):
    even = lax.axis_index(axis) % 2 == 0
    return jnp.where(even, upper, lower), jnp.where(even, lower, upper)


def all_sides(cells):
    return {
        "inline": sides_of(cells[0], cells[-1], "inline"),
        "xline": sides_of(cells[:, 0], cells[:, -1], "xline"),
    }


def harmonic_average(first, second):
    return 2.0 * first * second / (first + second)


def split2(value):
    high = value.astype(jnp.bfloat16)
    low = (value - high.astype(jnp.float32)).astype(jnp.bfloat16)
    return high, low


def dot_nt(a, b):
    return lax.dot_general(a, b, (((1,), (1,)), ((), ())), preferred_element_type=jnp.float32)


def dot_nn(a, b):
    return lax.dot_general(a, b, (((1,), (0,)), ((), ())), preferred_element_type=jnp.float32)


def one_hot(index_row, rows):
    shape = (rows, index_row.shape[1])
    return lax.broadcasted_iota(jnp.int32, shape, 0) == index_row


def well_place(owner_ref, well_ref, part):
    number = owner_ref[:, part] * WELL_DEV + well_ref[:, part]
    return number >> 7, number & (LANES - 1)


def fill_rows(cell_ref, row_ref):
    for start in range(0, cell_ref.shape[1], CHUNK):
        part = pl.ds(start, CHUNK)
        row_ref[:, part] = jnp.where(one_hot(cell_ref[:, part] >> 7, row_ref.shape[0]), 1.0, 0.0).astype(jnp.bfloat16)


def place_values(cell_ref, part, values, col_ref):
    hit = one_hot(cell_ref[:, part] & (LANES - 1), LANES)
    high, low = split2(values)
    col_ref[0:LANES, part] = jnp.where(hit, high.astype(jnp.float32), 0.0).astype(jnp.bfloat16)
    col_ref[LANES:, part] = jnp.where(hit, low.astype(jnp.float32), 0.0).astype(jnp.bfloat16)


def cells_sum(row_ref, col_ref):
    both = dot_nt(row_ref[...], col_ref[...])
    return both[:, :LANES] + both[:, LANES:]


def well_values(values, row, col, wells):
    hit = one_hot(row, wells)
    high, low = split2(values)
    weights = jnp.concatenate(
        [
            jnp.where(hit, high.astype(jnp.float32), 0.0),
            jnp.where(hit, low.astype(jnp.float32), 0.0),
        ],
        axis=0,
    ).astype(jnp.bfloat16)
    places = jnp.where(one_hot(col, LANES), 1.0, 0.0).astype(jnp.bfloat16)
    both = dot_nt(weights, places)
    return both[:wells] + both[wells:]


def gather_cells(fieldt, row_ref, cell_ref, part):
    both = dot_nn(fieldt, row_ref[:, part])
    picked = jnp.where(
        one_hot(cell_ref[:, part] & (LANES - 1), LANES), both[:LANES] + both[LANES:], 0.0
    )
    return jnp.sum(picked, axis=0, keepdims=True)


def gather_wells(table, row, col, wells):
    places = jnp.where(one_hot(col, LANES), 1.0, 0.0).astype(jnp.bfloat16)
    both = dot_nn(table, places)
    picked = jnp.where(one_hot(row, wells), both[:wells] + both[wells:], 0.0)
    return jnp.sum(picked, axis=0, keepdims=True)


def stack_split(value):
    high, low = split2(value)
    return jnp.concatenate([high.astype(jnp.float32), low.astype(jnp.float32)], axis=0).astype(jnp.bfloat16)


def lookup(facies, table_ref, row):
    result = jnp.full(facies.shape, table_ref[row, 0], jnp.float32)
    for entry in range(1, table_ref.shape[1]):
        result = jnp.where(facies == entry, table_ref[row, entry], result)
    return result


def lateral_kernel(table_ref, facies_ref, thickness_ref, lateral_ref):
    lateral_ref[...] = lookup(facies_ref[...], table_ref, 0) * thickness_ref[...]


def neighbours(cells, lower, upper, dim):
    if dim == 0:
        return (
            jnp.concatenate([lower[None], cells[:-1]], axis=0),
            jnp.concatenate([cells[1:], upper[None]], axis=0),
        )
    size = cells.shape[1]
    place = lax.broadcasted_iota(jnp.int32, cells.shape, 1)
    return (
        jnp.where(place == 0, lower[:, None], pltpu.roll(cells, 1, 1)),
        jnp.where(place == size - 1, upper[:, None], pltpu.roll(cells, size - 1, 1)),
    )


def layers(cells):
    return pltpu.roll(cells, 1, 2), pltpu.roll(cells, LANES - 1, 2)


def perforation_kernel(
    table_ref, facies_ref, thickness_ref, cell_ref, owner_ref, well_ref, index_ref,
    cellwi_ref, storage_ref, zlow_ref, zup_ref, row_ref, col_ref,
):
    vertical = lookup(facies_ref[...], table_ref, 1) / thickness_ref[...]
    below, above = layers(vertical)
    place = lax.broadcasted_iota(jnp.int32, vertical.shape, 2)
    zlow_ref[...] = jnp.where(place == 0, 0.0, harmonic_average(vertical, below))
    zup_ref[...] = jnp.where(place == LANES - 1, 0.0, harmonic_average(vertical, above))
    fill_rows(cell_ref, row_ref)
    total = jnp.zeros(storage_ref.shape, jnp.float32)
    for start in range(0, cell_ref.shape[1], CHUNK):
        part = pl.ds(start, CHUNK)
        place_values(cell_ref, part, index_ref[:, part], col_ref)
        row, col = well_place(owner_ref, well_ref, part)
        total = total + well_values(index_ref[:, part], row, col, storage_ref.shape[0])
    storage_ref[...] = total
    cellwi_ref[...] = cells_sum(row_ref, col_ref).reshape(cellwi_ref.shape)


def start_kernel(
    edge_ref, right_ref, lateral_ref, accumulation_ref, cellwi_ref, zlow_ref, zup_ref,
    ilow_ref, iup_ref, xlow_ref, xup_ref, cell_ref, owner_ref, well_ref, index_ref,
    til_ref, tiu_ref, txl_ref, txu_ref, diagonal_ref, inverse_ref, direction_ref, sums_ref, row_ref,
    *, scale,
):
    lateral = lateral_ref[...]
    low, up = neighbours(
        lateral,
        jnp.where(edge_ref[0] == 1, 0.0, ilow_ref[...]),
        jnp.where(edge_ref[1] == 1, 0.0, iup_ref[...]),
        0,
    )
    til, tiu = harmonic_average(lateral, low), harmonic_average(lateral, up)
    low, up = neighbours(
        lateral,
        jnp.where(edge_ref[2] == 1, 0.0, xlow_ref[...]),
        jnp.where(edge_ref[3] == 1, 0.0, xup_ref[...]),
        1,
    )
    txl, txu = harmonic_average(lateral, low), harmonic_average(lateral, up)
    til_ref[...], tiu_ref[...], txl_ref[...], txu_ref[...] = til, tiu, txl, txu
    diagonal = accumulation_ref[...] + til + tiu + txl + txu + zlow_ref[...] + zup_ref[...] + cellwi_ref[...]
    inverse = 1.0 / diagonal
    direction = right_ref[...] * inverse * scale
    diagonal_ref[...] = diagonal
    inverse_ref[...] = inverse
    direction_ref[...] = direction
    fill_rows(cell_ref, row_ref)
    sums_ref[...] = perforation_sums(direction, row_ref, cell_ref, owner_ref, well_ref, index_ref, sums_ref.shape[0])


def perforation_sums(direction, row_ref, cell_ref, owner_ref, well_ref, index_ref, wells):
    fieldt = stack_split(direction.reshape(-1, LANES).T)
    total = jnp.zeros((wells, LANES), jnp.float32)
    for start in range(0, cell_ref.shape[1], CHUNK):
        part = pl.ds(start, CHUNK)
        values = index_ref[:, part] * gather_cells(fieldt, row_ref, cell_ref, part)
        row, col = well_place(owner_ref, well_ref, part)
        total = total + well_values(values, row, col, wells)
    return total


def sweep_kernel(
    residual_ref, direction_ref, pressure_ref, diagonal_ref, inverse_ref,
    til_ref, tiu_ref, txl_ref, txu_ref, zlow_ref, zup_ref,
    ilow_ref, iup_ref, xlow_ref, xup_ref, sums_ref, storage_ref,
    cell_ref, owner_ref, well_ref, index_ref,
    *rest, keep, gain, first,
):
    last = keep is None
    if last:
        next_pressure_ref, next_residual_ref, row_ref, col_ref = rest
    else:
        next_pressure_ref, next_residual_ref, next_direction_ref, next_sums_ref, row_ref, col_ref = rest
    wells = sums_ref.shape[0]
    fill_rows(cell_ref, row_ref)
    bottom = stack_split(sums_ref[...] / (1.0 + storage_ref[...]))
    for start in range(0, cell_ref.shape[1], CHUNK):
        part = pl.ds(start, CHUNK)
        row, col = well_place(owner_ref, well_ref, part)
        values = index_ref[:, part] * gather_wells(bottom, row, col, wells)
        place_values(cell_ref, part, values, col_ref)
    direction = direction_ref[...]
    ilow, iup = neighbours(direction, ilow_ref[...], iup_ref[...], 0)
    xlow, xup = neighbours(direction, xlow_ref[...], xup_ref[...], 1)
    below, above = layers(direction)
    beside = (
        til_ref[...] * ilow + tiu_ref[...] * iup + txl_ref[...] * xlow + txu_ref[...] * xup
        + zlow_ref[...] * below + zup_ref[...] * above
    )
    wells_term = cells_sum(row_ref, col_ref).reshape(direction.shape)
    residual = residual_ref[...] - (diagonal_ref[...] * direction - beside - wells_term)
    next_residual_ref[...] = residual
    if first:
        next_pressure_ref[...] = direction
    else:
        next_pressure_ref[...] = pressure_ref[...] + direction
    if not last:
        following = keep * direction + gain * (residual * inverse_ref[...])
        next_direction_ref[...] = following
        next_sums_ref[...] = perforation_sums(
            following, row_ref, cell_ref, owner_ref, well_ref, index_ref, wells
        )


def body(
    right_side,
    facies,
    facies_table,
    thickness,
    accumulation,
    perforation_cell,
    perf_owner,
    perf_well,
    perf_index,
):
    shape = right_side.shape
    f32 = jnp.float32
    grid = jax.ShapeDtypeStruct(shape, f32)
    n_perf = perforation_cell.shape[0]
    n_dev = lax.axis_size("inline") * lax.axis_size("xline")
    wells = -(-n_dev * WELL_DEV // (8 * LANES)) * 8
    sums = jax.ShapeDtypeStruct((wells, LANES), f32)
    cell = perforation_cell.reshape(1, n_perf)
    owner = perf_owner.reshape(1, n_perf)
    well = perf_well.reshape(1, n_perf)
    index = perf_index.reshape(1, n_perf)
    perforations = (cell, owner, well, index)
    rows = shape[0] * shape[1]
    row_scratch = pltpu.VMEM((rows, n_perf), jnp.bfloat16)
    col_scratch = pltpu.VMEM((2 * LANES, n_perf), jnp.bfloat16)

    lateral = pl.pallas_call(
        lateral_kernel, out_shape=grid, in_specs=[SMEM, VMEM, VMEM], out_specs=VMEM,
    )(facies_table, facies, thickness)
    lateral_halo = side_exchange(all_sides(lateral))
    cellwi, storage, zlow, zup = pl.pallas_call(
        perforation_kernel,
        out_shape=(grid, sums, grid, grid),
        in_specs=[SMEM] + [VMEM] * 6,
        out_specs=(VMEM,) * 4,
        scratch_shapes=[row_scratch, col_scratch],
        compiler_params=PARAMS,
    )(facies_table, facies, thickness, *perforations)

    gi, gx = lax.axis_index("inline"), lax.axis_index("xline")
    edges = jnp.stack(
        [gi == 0, gi == lax.axis_size("inline") - 1, gx == 0, gx == lax.axis_size("xline") - 1]
    ).astype(jnp.int32)

    theta = (HIGH_BOUND + LOW_BOUND) / 2.0
    delta = (HIGH_BOUND - LOW_BOUND) / 2.0
    sigma = theta / delta
    rho_now = 1.0 / sigma
    til, tiu, txl, txu, diagonal, inverse, direction, partial = pl.pallas_call(
        functools.partial(start_kernel, scale=1.0 / theta),
        out_shape=(grid,) * 7 + (sums,),
        in_specs=[SMEM] + [VMEM] * 14,
        out_specs=(VMEM,) * 8,
        scratch_shapes=[row_scratch],
        compiler_params=PARAMS,
    )(edges, right_side, lateral, accumulation, cellwi, zlow, zup,
      *lateral_halo["inline"], *lateral_halo["xline"], *perforations)

    residual, pressure = right_side, right_side
    for sweep in range(SWEEPS):
        last = sweep + 1 == SWEEPS
        if sweep == 0:
            both, halo = all_sum(jnp.concatenate([partial, storage], axis=0), all_sides(direction))
            total, storage = both[:wells], both[wells:]
        else:
            total, halo = all_sum(partial, all_sides(direction))
        keep = gain = None
        if not last:
            rho_next = 1.0 / (2.0 * sigma - rho_now)
            keep, gain = rho_next * rho_now, 2.0 * rho_next / delta
            rho_now = rho_next
        results = pl.pallas_call(
            functools.partial(sweep_kernel, keep=keep, gain=gain, first=sweep == 0),
            out_shape=(grid, grid) if last else (grid, grid, grid, sums),
            in_specs=[VMEM] * 21,
            out_specs=(VMEM,) * (2 if last else 4),
            scratch_shapes=[row_scratch, col_scratch],
            compiler_params=PARAMS,
        )(residual, direction, pressure, diagonal, inverse, til, tiu, txl, txu, zlow, zup,
          *halo["inline"], *halo["xline"], total, storage, *perforations)
        if last:
            pressure, residual = results
        else:
            pressure, residual, direction, partial = results
    return pressure, residual


def solution(mesh):
    in_specs = (
        P("inline", "xline", None),
        P("inline", "xline", None),
        P(),
        P("inline", "xline", None),
        P("inline", "xline", None),
        P(("inline", "xline")),
        P(("inline", "xline"), None),
        P(("inline", "xline")),
        P(("inline", "xline")),
    )
    out_specs = (P("inline", "xline", None), P("inline", "xline", None))
    return jax.shard_map(body, mesh=mesh, in_specs=in_specs, out_specs=out_specs, check_vma=False)
```

```python
import functools

import jax
import jax.numpy as jnp
from jax import lax
from jax.experimental import pallas as pl
from jax.experimental.pallas import tpu as pltpu
from jax.sharding import PartitionSpec as P

SWEEPS = 3
WELL_DEV = 160
LANES = 128
LOW_BOUND = 0.1
HIGH_BOUND = 2.0
CHUNK = 512
MESH_AXES = ("inline", "xline")

VMEM = pl.BlockSpec(memory_space=pltpu.VMEM)
HBM = pl.BlockSpec(memory_space=pltpu.HBM)
PARAMS = pltpu.CompilerParams(vmem_limit_bytes=16 * 1024 * 1024)
SMALL = pltpu.CompilerParams(vmem_limit_bytes=4 * 1024 * 1024)


def pair_permute(value, partner):
    ni, nx = lax.axis_size("inline"), lax.axis_size("xline")
    pairs = []
    for i in range(ni):
        for j in range(nx):
            i2, j2 = partner(i, j)
            pairs.append((i * nx + j, i2 * nx + j2))
    return lax.ppermute(value, MESH_AXES, pairs)


def xor_permute(value, inline_mask, xline_mask):
    return pair_permute(value, lambda i, j: (i ^ inline_mask, j ^ xline_mask))


def bits_of(count):
    bits = count.bit_length() - 1
    if 1 << bits != count:
        raise ValueError("axis size")
    return bits


def side_masks(count):
    return [(2 << s) - 1 for s in range(bits_of(count))]


def stages_of(count):
    bits = bits_of(count)
    cuts = ([1] if bits % 2 else []) + [2] * (bits // 2)
    stages, low = [], 0
    for width in cuts:
        stages.append([pattern << low | (1 << low) - 1 for pattern in range(1, 1 << width)])
        low += width
    return stages


def all_sum(value, sides):
    arrived = {}
    rows = value.shape[0]
    xa, xb = sides["xline"]
    mates = None
    for masks in stages_of(lax.axis_size("xline")):
        total = value
        for mask in masks:
            if mask == 1:
                got = xor_permute(jnp.concatenate([value, xa, *sides["inline"]], axis=0), 0, mask)
                lines = xa.shape[0]
                arrived["xline", mask] = got[rows : rows + lines]
                mates = jnp.split(got[rows + lines :], 2, axis=0)
            elif mask in side_masks(lax.axis_size("xline")):
                got = xor_permute(jnp.concatenate([value, xb], axis=0), 0, mask)
                arrived["xline", mask] = got[rows:]
            else:
                got = xor_permute(value, 0, mask)
            total = total + got[:rows]
        value = total
    for masks in stages_of(lax.axis_size("inline")):
        total = value
        for mask in masks:
            if mask in side_masks(lax.axis_size("inline")):
                face = mates[0 if mask == 1 else 1]
                got = xor_permute(jnp.concatenate([value, face], axis=0), mask, 1)
                arrived["inline", mask] = got[rows:]
            else:
                got = xor_permute(value, mask, 1)
            total = total + got[:rows]
        value = total
    return value, halos(arrived)


def beyond(index, count):
    other = index - 1 if index % 2 == 0 else index + 1
    return other if 0 <= other < count else None


def side_exchange(sides):
    ni, nx = lax.axis_size("inline"), lax.axis_size("xline")

    def inline_far(i, j):
        other = beyond(i, ni)
        return (i, j ^ 1) if other is None else (other, j)

    def xline_far(i, j):
        other = beyond(j, nx)
        return (i ^ 1, j) if other is None else (i, other)

    return {
        "inline": ordered("inline", xor_permute(sides["inline"][0], 1, 0), pair_permute(sides["inline"][1], inline_far)),
        "xline": ordered("xline", xor_permute(sides["xline"][0], 0, 1), pair_permute(sides["xline"][1], xline_far)),
    }


def ordered(axis, beside, far):
    even = lax.axis_index(axis) % 2 == 0
    return jnp.where(even, far, beside), jnp.where(even, beside, far)


def halos(arrived):
    result = {}
    for axis in MESH_AXES:
        index = lax.axis_index(axis)
        other = jnp.where(index % 2 == 0, index - 1, index + 1)
        far = arrived[axis, 1]
        for mask in side_masks(lax.axis_size(axis))[1:]:
            far = jnp.where((index ^ other) == mask, arrived[axis, mask], far)
        result[axis] = ordered(axis, arrived[axis, 1], far)
    return result


def sides_of(lower, upper, axis):
    even = lax.axis_index(axis) % 2 == 0
    return jnp.where(even, upper, lower), jnp.where(even, lower, upper)


def all_sides(cells):
    return {
        "inline": sides_of(cells[0], cells[-1], "inline"),
        "xline": sides_of(cells[:, 0], cells[:, -1], "xline"),
    }


def harmonic_average(first, second):
    return 2.0 * first * second / (first + second)


def split2(value):
    high = value.astype(jnp.bfloat16)
    low = (value - high.astype(jnp.float32)).astype(jnp.bfloat16)
    return high, low


def stack_split(value):
    return jnp.concatenate(split2(value), axis=0)


def dot_nt(a, b):
    return lax.dot_general(a, b, (((1,), (1,)), ((), ())), preferred_element_type=jnp.float32)


def dot_nn(a, b):
    return lax.dot_general(a, b, (((1,), (0,)), ((), ())), preferred_element_type=jnp.float32)


def halves_sum(both):
    half = both.shape[0] // 2
    return both[:half] + both[half:]


def one_hot(index_row, rows):
    shape = (rows, index_row.shape[1])
    hit = lax.broadcasted_iota(jnp.int32, shape, 0) == index_row
    return jnp.where(hit, 1.0, 0.0).astype(jnp.bfloat16)


def scaled(hot, values):
    rows, count = hot.shape
    tiles = hot.reshape(rows // 16, 16, count)
    pieces = split2(jnp.broadcast_to(values, (16, count)))
    return [(tiles * piece[None]).reshape(rows, count) for piece in pieces]


def picked_sum(hot, values):
    return jnp.sum(hot.astype(jnp.float32) * values, axis=0, keepdims=True)


def parts(count):
    return [pl.ds(start, CHUNK) for start in range(0, count, CHUNK)]


def lookup(facies, table_ref, row):
    result = jnp.full(facies.shape, table_ref[row, 0], jnp.float32)
    for entry in range(1, table_ref.shape[1]):
        result = jnp.where(facies == entry, table_ref[row, entry], result)
    return result


def neighbours(cells, lower, upper, dim):
    if dim == 0:
        return (
            jnp.concatenate([lower[None], cells[:-1]], axis=0),
            jnp.concatenate([cells[1:], upper[None]], axis=0),
        )
    size = cells.shape[1]
    place = lax.broadcasted_iota(jnp.int32, cells.shape, 1)
    return (
        jnp.where(place == 0, lower[:, None], pltpu.roll(cells, 1, 1)),
        jnp.where(place == size - 1, upper[:, None], pltpu.roll(cells, size - 1, 1)),
    )


def layers(cells):
    return pltpu.roll(cells, 1, 2), pltpu.roll(cells, LANES - 1, 2)


def load_kernel(
    table_hbm, facies_hbm, thickness_hbm, right_hbm, accumulation_hbm, cell_hbm, owner_hbm, well_hbm, index_hbm,
    ia_ref, ib_ref, xa_ref, xb_ref, lateral_ref, vertical_ref,
    right_ref, accumulation_ref, cell_ref, number_ref, index_ref,
    table_ref, facies_ref, thickness_ref, owner_ref, well_ref, sems,
):
    copies = [
        pltpu.make_async_copy(source, target, sems.at[slot])
        for slot, (source, target) in enumerate(
            (
                (table_hbm, table_ref), (facies_hbm, facies_ref), (thickness_hbm, thickness_ref),
                (owner_hbm, owner_ref), (well_hbm, well_ref), (right_hbm, right_ref),
                (accumulation_hbm, accumulation_ref), (cell_hbm, cell_ref), (index_hbm, index_ref),
            )
        )
    ]
    for copy in copies:
        copy.start()
    for copy in copies:
        copy.wait()
    facies, thickness = facies_ref[...], thickness_ref[...]
    lateral = lookup(facies, table_ref, 0) * thickness
    lateral_ref[...] = lateral
    vertical_ref[...] = lookup(facies, table_ref, 1) / thickness
    for axis, lower, upper, a_ref, b_ref in (
        ("inline", lateral[0], lateral[-1], ia_ref, ib_ref),
        ("xline", lateral[:, 0], lateral[:, -1], xa_ref, xb_ref),
    ):
        odd = lax.axis_index(axis) % 2 == 1
        a_ref[...] = jnp.where(odd, lower, upper)
        b_ref[...] = jnp.where(odd, upper, lower)
    number_ref[...] = owner_ref[...] * WELL_DEV + well_ref[...]


def perforation_kernel(
    vertical_ref, cell_ref, number_ref, index_ref,
    cellwi_ref, storage_ref, zlow_ref, zup_ref, row_ref, col_ref, wrow_ref, wcol_ref, scaled_ref,
):
    vertical = vertical_ref[...]
    below, above = layers(vertical)
    place = lax.broadcasted_iota(jnp.int32, vertical.shape, 2)
    zlow_ref[...] = jnp.where(place == 0, 0.0, harmonic_average(vertical, below))
    zup_ref[...] = jnp.where(place == LANES - 1, 0.0, harmonic_average(vertical, above))
    for part in parts(cell_ref.shape[1]):
        cell, number = cell_ref[:, part], number_ref[:, part]
        row_ref[:, part] = one_hot(cell >> 7, row_ref.shape[0])
        col_ref[:, part] = one_hot(cell & (LANES - 1), LANES)
        wrow_ref[:, part] = one_hot(number >> 7, wrow_ref.shape[0])
        wcol_ref[:, part] = one_hot(number & (LANES - 1), LANES)
    cellwi_ref[...] = cells_sum(index_ref, row_ref, col_ref, scaled_ref).reshape(cellwi_ref.shape)
    total = 0.0
    for part in parts(cell_ref.shape[1]):
        total = total + wells_sum(index_ref[:, part], wrow_ref, wcol_ref, part)
    storage_ref[...] = total[: storage_ref.shape[0]]


def put_scaled(values, col_ref, scaled_ref, part):
    scaled_ref[0:LANES, part], scaled_ref[LANES:, part] = scaled(col_ref[:, part], values)


def cells_sum(values_ref, row_ref, col_ref, scaled_ref):
    if values_ref is not None:
        for part in parts(row_ref.shape[1]):
            put_scaled(values_ref[:, part], col_ref, scaled_ref, part)
    both = dot_nt(row_ref[...], scaled_ref[...])
    return both[:, :LANES] + both[:, LANES:]


def wells_sum(values, wrow_ref, wcol_ref, part):
    pieces = scaled(wrow_ref[:, part], values)
    return halves_sum(dot_nt(jnp.concatenate(pieces, axis=0), wcol_ref[:, part]))


def perforation_sums(direction, row_ref, col_ref, wrow_ref, wcol_ref, index_ref, wells):
    fieldt = stack_split(direction.reshape(-1, LANES).T)
    total = 0.0
    for part in parts(row_ref.shape[1]):
        values = picked_sum(col_ref[:, part], halves_sum(dot_nn(fieldt, row_ref[:, part])))
        total = total + wells_sum(index_ref[:, part] * values, wrow_ref, wcol_ref, part)
    return total[:wells]


def start_kernel(
    right_ref, lateral_ref, accumulation_ref, cellwi_ref, zlow_ref, zup_ref,
    ilow_ref, iup_ref, xlow_ref, xup_ref, row_ref, col_ref, wrow_ref, wcol_ref, index_ref,
    til_ref, tiu_ref, txl_ref, txu_ref, diagonal_ref, inverse_ref, direction_ref, sums_ref,
    *, scale,
):
    lateral = lateral_ref[...]
    gi, gx = lax.axis_index("inline"), lax.axis_index("xline")
    low, up = neighbours(
        lateral,
        jnp.where(gi == 0, 0.0, ilow_ref[...]),
        jnp.where(gi == lax.axis_size("inline") - 1, 0.0, iup_ref[...]),
        0,
    )
    til, tiu = harmonic_average(lateral, low), harmonic_average(lateral, up)
    low, up = neighbours(
        lateral,
        jnp.where(gx == 0, 0.0, xlow_ref[...]),
        jnp.where(gx == lax.axis_size("xline") - 1, 0.0, xup_ref[...]),
        1,
    )
    txl, txu = harmonic_average(lateral, low), harmonic_average(lateral, up)
    til_ref[...], tiu_ref[...], txl_ref[...], txu_ref[...] = til, tiu, txl, txu
    diagonal = accumulation_ref[...] + til + tiu + txl + txu + zlow_ref[...] + zup_ref[...] + cellwi_ref[...]
    inverse = 1.0 / diagonal
    direction = right_ref[...] * inverse * scale
    diagonal_ref[...] = diagonal
    inverse_ref[...] = inverse
    direction_ref[...] = direction
    sums_ref[...] = perforation_sums(direction, row_ref, col_ref, wrow_ref, wcol_ref, index_ref, sums_ref.shape[0])


def sweep_kernel(
    residual_ref, direction_ref, pressure_ref, diagonal_ref, inverse_ref,
    til_ref, tiu_ref, txl_ref, txu_ref, zlow_ref, zup_ref,
    ilow_ref, iup_ref, xlow_ref, xup_ref, sums_ref, storage_ref,
    row_ref, col_ref, wrow_ref, wcol_ref, index_ref,
    *rest, keep, gain, first,
):
    last = keep is None
    if last:
        next_pressure_ref, next_residual_ref, scaled_ref = rest
    else:
        next_pressure_ref, next_residual_ref, next_direction_ref, next_sums_ref, scaled_ref = rest
    wells = sums_ref.shape[0]
    bottom = sums_ref[...] / (1.0 + storage_ref[...])
    spare = wrow_ref.shape[0] - wells
    if spare:
        bottom = jnp.concatenate([bottom, jnp.zeros((spare, LANES), jnp.float32)], axis=0)
    table = stack_split(bottom)
    for part in parts(row_ref.shape[1]):
        values = picked_sum(wrow_ref[:, part], halves_sum(dot_nn(table, wcol_ref[:, part])))
        put_scaled(index_ref[:, part] * values, col_ref, scaled_ref, part)
    direction = direction_ref[...]
    ilow, iup = neighbours(direction, ilow_ref[...], iup_ref[...], 0)
    xlow, xup = neighbours(direction, xlow_ref[...], xup_ref[...], 1)
    below, above = layers(direction)
    beside = (
        til_ref[...] * ilow + tiu_ref[...] * iup + txl_ref[...] * xlow + txu_ref[...] * xup
        + zlow_ref[...] * below + zup_ref[...] * above
    )
    wells_term = cells_sum(None, row_ref, col_ref, scaled_ref).reshape(direction.shape)
    residual = residual_ref[...] - (diagonal_ref[...] * direction - beside - wells_term)
    next_residual_ref[...] = residual
    if first:
        next_pressure_ref[...] = direction
    else:
        next_pressure_ref[...] = pressure_ref[...] + direction
    if not last:
        following = keep * direction + gain * (residual * inverse_ref[...])
        next_direction_ref[...] = following
        next_sums_ref[...] = perforation_sums(following, row_ref, col_ref, wrow_ref, wcol_ref, index_ref, wells)


def body(
    right_side,
    facies,
    facies_table,
    thickness,
    accumulation,
    perforation_cell,
    perf_owner,
    perf_well,
    perf_index,
):
    shape = right_side.shape
    f32 = jnp.float32
    grid = jax.ShapeDtypeStruct(shape, f32)
    n_perf = perforation_cell.shape[0]
    n_dev = lax.axis_size("inline") * lax.axis_size("xline")
    wells = -(-n_dev * WELL_DEV // (8 * LANES)) * 8
    wells_hot = -(-wells // 16) * 16
    sums = jax.ShapeDtypeStruct((wells, LANES), f32)
    faces = [jax.ShapeDtypeStruct((size, LANES), f32) for size in (shape[1], shape[1], shape[0], shape[0])]
    cell = perforation_cell.reshape(1, n_perf)
    owner = perf_owner.reshape(1, n_perf)
    well = perf_well.reshape(1, n_perf)
    index = perf_index.reshape(1, n_perf)
    rows = shape[0] * shape[1]
    hots = tuple(jax.ShapeDtypeStruct((size, n_perf), jnp.bfloat16) for size in (rows, LANES, wells_hot, LANES))
    scaled_scratch = pltpu.VMEM((2 * LANES, n_perf), jnp.bfloat16)

    row_i32 = jax.ShapeDtypeStruct((1, n_perf), jnp.int32)
    row_f32 = jax.ShapeDtypeStruct((1, n_perf), f32)
    ia, ib, xa, xb, lateral, vertical, right_side, accumulation, cell, number, index = pl.pallas_call(
        load_kernel,
        out_shape=(*faces, grid, grid, grid, grid, row_i32, row_i32, row_f32),
        in_specs=[HBM] * 9,
        out_specs=(VMEM,) * 11,
        scratch_shapes=[
            pltpu.SMEM(facies_table.shape, f32),
            pltpu.VMEM(shape, jnp.int32),
            pltpu.VMEM(shape, f32),
            pltpu.VMEM((1, n_perf), jnp.int32),
            pltpu.VMEM((1, n_perf), jnp.int32),
            pltpu.SemaphoreType.DMA((9,)),
        ],
        compiler_params=SMALL,
    )(*(
        pltpu.with_memory_space_constraint(value, pltpu.HBM)
        for value in (facies_table, facies, thickness, right_side, accumulation, cell, owner, well, index)
    ))
    lateral_halo = side_exchange({"inline": (ia, ib), "xline": (xa, xb)})
    cellwi, storage, zlow, zup, *hot = pl.pallas_call(
        perforation_kernel,
        out_shape=(grid, sums, grid, grid, *hots),
        in_specs=[VMEM] * 4,
        out_specs=(VMEM,) * 8,
        scratch_shapes=[scaled_scratch],
        compiler_params=PARAMS,
    )(vertical, cell, number, index)

    theta = (HIGH_BOUND + LOW_BOUND) / 2.0
    delta = (HIGH_BOUND - LOW_BOUND) / 2.0
    sigma = theta / delta
    rho_now = 1.0 / sigma
    til, tiu, txl, txu, diagonal, inverse, direction, partial = pl.pallas_call(
        functools.partial(start_kernel, scale=1.0 / theta),
        out_shape=(grid,) * 7 + (sums,),
        in_specs=[VMEM] * 15,
        out_specs=(VMEM,) * 8,
        compiler_params=PARAMS,
    )(right_side, lateral, accumulation, cellwi, zlow, zup,
      *lateral_halo["inline"], *lateral_halo["xline"], *hot, index)

    residual, pressure = right_side, right_side
    for sweep in range(SWEEPS):
        last = sweep + 1 == SWEEPS
        if sweep == 0:
            both, halo = all_sum(jnp.concatenate([partial, storage], axis=0), all_sides(direction))
            total, storage = both[:wells], both[wells:]
        else:
            total, halo = all_sum(partial, all_sides(direction))
        keep = gain = None
        if not last:
            rho_next = 1.0 / (2.0 * sigma - rho_now)
            keep, gain = rho_next * rho_now, 2.0 * rho_next / delta
            rho_now = rho_next
        results = pl.pallas_call(
            functools.partial(sweep_kernel, keep=keep, gain=gain, first=sweep == 0),
            out_shape=(grid, grid) if last else (grid, grid, grid, sums),
            in_specs=[VMEM] * 22,
            out_specs=(VMEM,) * (2 if last else 4),
            scratch_shapes=[scaled_scratch],
            compiler_params=PARAMS,
        )(residual, direction, pressure, diagonal, inverse, til, tiu, txl, txu, zlow, zup,
          *halo["inline"], *halo["xline"], total, storage, *hot, index)
        if last:
            pressure, residual = results
        else:
            pressure, residual, direction, partial = results
    return pressure, residual


def solution(mesh):
    in_specs = (
        P("inline", "xline", None),
        P("inline", "xline", None),
        P(),
        P("inline", "xline", None),
        P("inline", "xline", None),
        P(("inline", "xline")),
        P(("inline", "xline"), None),
        P(("inline", "xline")),
        P(("inline", "xline")),
    )
    out_specs = (P("inline", "xline", None), P("inline", "xline", None))
    return jax.shard_map(body, mesh=mesh, in_specs=in_specs, out_specs=out_specs, check_vma=False)
```

```python
import functools

import jax
import jax.numpy as jnp
from jax import lax
from jax.experimental import pallas as pl
from jax.experimental.pallas import tpu as pltpu
from jax.sharding import PartitionSpec as P

SWEEPS = 3
WELL_DEV = 160
LANES = 128
LOW_BOUND = 0.1
HIGH_BOUND = 2.0
CHUNK = 512
MESH_AXES = ("inline", "xline")

VMEM = pl.BlockSpec(memory_space=pltpu.VMEM)
HBM = pl.BlockSpec(memory_space=pltpu.HBM)
PARAMS = pltpu.CompilerParams(vmem_limit_bytes=16 * 1024 * 1024)
SMALL = pltpu.CompilerParams(vmem_limit_bytes=4 * 1024 * 1024)


def pair_permute(value, partner):
    ni, nx = lax.axis_size("inline"), lax.axis_size("xline")
    pairs = []
    for i in range(ni):
        for j in range(nx):
            i2, j2 = partner(i, j)
            pairs.append((i * nx + j, i2 * nx + j2))
    return lax.ppermute(value, MESH_AXES, pairs)


def xor_permute(value, inline_mask, xline_mask):
    return pair_permute(value, lambda i, j: (i ^ inline_mask, j ^ xline_mask))


def bits_of(count):
    bits = count.bit_length() - 1
    if 1 << bits != count:
        raise ValueError("axis size")
    return bits


def side_masks(count):
    return [(2 << s) - 1 for s in range(bits_of(count))]


def stages_of(count):
    bits = bits_of(count)
    cuts = ([1] if bits % 2 else []) + [2] * (bits // 2)
    stages, low = [], 0
    for width in cuts:
        stages.append([pattern << low | (1 << low) - 1 for pattern in range(1, 1 << width)])
        low += width
    return stages


def all_stages():
    return [[(0, mask) for mask in masks] for masks in stages_of(lax.axis_size("xline"))] + [
        [(mask, 1) for mask in masks] for masks in stages_of(lax.axis_size("inline"))
    ]


SPLIT_STAGES = [[(0, 1)], [(0, 3), (0, 4), (0, 7)], [(1, 1), (2, 0), (3, 1)]]


def exchange_stage(value, stage, riders, arrived):
    rows = value.shape[0]
    total = value
    for masks in stage:
        rider = riders.get(masks)
        if rider is None:
            got = xor_permute(value, *masks)
        else:
            got = xor_permute(jnp.concatenate([value, rider], axis=0), *masks)
            arrived[masks] = got[rows:]
        total = total + got[:rows]
    return total


def all_sum(value, sides):
    ni, nx = lax.axis_size("inline"), lax.axis_size("xline")
    xa, xb = sides["xline"]
    first, *others = all_stages()
    split = isinstance(value, tuple)
    if split:
        halves = [part.shape[0] for part in value]
        value = jnp.concatenate(value, axis=0)
        if len(first) == 1 and [len(stage) for stage in others] == [3, 3] and halves[0] == halves[1]:
            others = SPLIT_STAGES[1:]
            two_kinds = True
        else:
            two_kinds = False
    arrived = {}
    riders = {(0, mask): xb for mask in side_masks(nx)}
    riders[0, 1] = jnp.concatenate([xa, *sides["inline"]], axis=0)
    value = exchange_stage(value, first, riders, arrived)
    beside, mate_a, mate_b = jnp.split(
        arrived[0, 1], [xa.shape[0], xa.shape[0] + sides["inline"][0].shape[0]], axis=0
    )
    arrived[0, 1] = beside
    del riders[0, 1]
    for mask in side_masks(ni):
        riders[mask, 1] = mate_a if mask == 1 else mate_b
    if split and two_kinds:
        gi, gx = lax.axis_index("inline"), lax.axis_index("xline")
        kind = (gx ^ (gx >> 1) ^ gi) & 1
        value = jnp.where(kind == 0, value[: halves[0]], value[halves[0] :])
    for stage in others:
        value = exchange_stage(value, stage, riders, arrived)
    if split:
        if two_kinds:
            swapped = xor_permute(value, 0, 1)
            value = (jnp.where(kind == 0, value, swapped), jnp.where(kind == 0, swapped, value))
        else:
            value = (value[: halves[0]], value[halves[0] :])
    return value, halos(
        {
            "inline": {mask: arrived[mask, 1] for mask in side_masks(ni)},
            "xline": {mask: arrived[0, mask] for mask in side_masks(nx)},
        }
    )


def beyond(index, count):
    other = index - 1 if index % 2 == 0 else index + 1
    return other if 0 <= other < count else None


def side_exchange(sides):
    ni, nx = lax.axis_size("inline"), lax.axis_size("xline")

    def inline_far(i, j):
        other = beyond(i, ni)
        return (i, j ^ 1) if other is None else (other, j)

    def xline_far(i, j):
        other = beyond(j, nx)
        return (i ^ 1, j) if other is None else (i, other)

    return {
        "inline": ordered("inline", xor_permute(sides["inline"][0], 1, 0), pair_permute(sides["inline"][1], inline_far)),
        "xline": ordered("xline", xor_permute(sides["xline"][0], 0, 1), pair_permute(sides["xline"][1], xline_far)),
    }


def ordered(axis, beside, far):
    even = lax.axis_index(axis) % 2 == 0
    return jnp.where(even, far, beside), jnp.where(even, beside, far)


def halos(arrived):
    result = {}
    for axis in MESH_AXES:
        index = lax.axis_index(axis)
        other = jnp.where(index % 2 == 0, index - 1, index + 1)
        far = arrived[axis][1]
        for mask in side_masks(lax.axis_size(axis))[1:]:
            far = jnp.where((index ^ other) == mask, arrived[axis][mask], far)
        result[axis] = ordered(axis, arrived[axis][1], far)
    return result


def sides_of(lower, upper, axis):
    even = lax.axis_index(axis) % 2 == 0
    return jnp.where(even, upper, lower), jnp.where(even, lower, upper)


def all_sides(cells):
    return {
        "inline": sides_of(cells[0], cells[-1], "inline"),
        "xline": sides_of(cells[:, 0], cells[:, -1], "xline"),
    }


def harmonic_average(first, second):
    return 2.0 * first * second / (first + second)


def split2(value):
    high = value.astype(jnp.bfloat16)
    low = (value - high.astype(jnp.float32)).astype(jnp.bfloat16)
    return high, low


def stack_split(value):
    return jnp.concatenate(split2(value), axis=0)


def dot_nt(a, b):
    return lax.dot_general(a, b, (((1,), (1,)), ((), ())), preferred_element_type=jnp.float32)


def dot_nn(a, b):
    return lax.dot_general(a, b, (((1,), (0,)), ((), ())), preferred_element_type=jnp.float32)


def halves_sum(both):
    half = both.shape[0] // 2
    return both[:half] + both[half:]


def one_hot(index_row, rows):
    shape = (rows, index_row.shape[1])
    hit = lax.broadcasted_iota(jnp.int32, shape, 0) == index_row
    return jnp.where(hit, 1.0, 0.0).astype(jnp.bfloat16)


def scaled(hot, values):
    rows, count = hot.shape
    tiles = hot.reshape(rows // 16, 16, count)
    pieces = split2(jnp.broadcast_to(values, (16, count)))
    return [(tiles * piece[None]).reshape(rows, count) for piece in pieces]


def picked_sum(hot, values):
    return jnp.sum(hot.astype(jnp.float32) * values, axis=0, keepdims=True)


def parts(count):
    return [pl.ds(start, CHUNK) for start in range(0, count, CHUNK)]


def lookup(facies, table_ref, row):
    result = jnp.full(facies.shape, table_ref[row, 0], jnp.float32)
    for entry in range(1, table_ref.shape[1]):
        result = jnp.where(facies == entry, table_ref[row, entry], result)
    return result


def neighbours(cells, lower, upper, dim):
    if dim == 0:
        return (
            jnp.concatenate([lower[None], cells[:-1]], axis=0),
            jnp.concatenate([cells[1:], upper[None]], axis=0),
        )
    size = cells.shape[1]
    place = lax.broadcasted_iota(jnp.int32, cells.shape, 1)
    return (
        jnp.where(place == 0, lower[:, None], pltpu.roll(cells, 1, 1)),
        jnp.where(place == size - 1, upper[:, None], pltpu.roll(cells, size - 1, 1)),
    )


def layers(cells):
    return pltpu.roll(cells, 1, 2), pltpu.roll(cells, LANES - 1, 2)


def load_kernel(
    table_hbm, facies_hbm, thickness_hbm, right_hbm, accumulation_hbm, cell_hbm, owner_hbm, well_hbm, index_hbm,
    ia_ref, ib_ref, xa_ref, xb_ref, lateral_ref, vertical_ref,
    right_ref, accumulation_ref, cell_ref, number_ref, index_ref,
    table_ref, facies_ref, thickness_ref, owner_ref, well_ref, sems,
):
    copies = [
        pltpu.make_async_copy(source, target, sems.at[slot])
        for slot, (source, target) in enumerate(
            (
                (table_hbm, table_ref), (facies_hbm, facies_ref), (thickness_hbm, thickness_ref),
                (owner_hbm, owner_ref), (well_hbm, well_ref), (right_hbm, right_ref),
                (accumulation_hbm, accumulation_ref), (cell_hbm, cell_ref), (index_hbm, index_ref),
            )
        )
    ]
    for copy in copies:
        copy.start()
    for copy in copies:
        copy.wait()
    facies, thickness = facies_ref[...], thickness_ref[...]
    lateral = lookup(facies, table_ref, 0) * thickness
    lateral_ref[...] = lateral
    vertical_ref[...] = lookup(facies, table_ref, 1) / thickness
    for axis, lower, upper, a_ref, b_ref in (
        ("inline", lateral[0], lateral[-1], ia_ref, ib_ref),
        ("xline", lateral[:, 0], lateral[:, -1], xa_ref, xb_ref),
    ):
        odd = lax.axis_index(axis) % 2 == 1
        a_ref[...] = jnp.where(odd, lower, upper)
        b_ref[...] = jnp.where(odd, upper, lower)
    number_ref[...] = owner_ref[...] * WELL_DEV + well_ref[...]


def perforation_kernel(
    vertical_ref, cell_ref, number_ref, index_ref,
    cellwi_ref, storage_ref, zlow_ref, zup_ref, row_ref, col_ref, wrow_ref, wcol_ref, scaled_ref, wscaled_ref,
):
    vertical = vertical_ref[...]
    below, above = layers(vertical)
    place = lax.broadcasted_iota(jnp.int32, vertical.shape, 2)
    zlow_ref[...] = jnp.where(place == 0, 0.0, harmonic_average(vertical, below))
    zup_ref[...] = jnp.where(place == LANES - 1, 0.0, harmonic_average(vertical, above))
    for part in parts(cell_ref.shape[1]):
        cell, number = cell_ref[:, part], number_ref[:, part]
        row_ref[:, part] = one_hot(cell >> 7, row_ref.shape[0])
        col_ref[:, part] = one_hot(cell & (LANES - 1), LANES)
        wrow_ref[:, part] = one_hot(number >> 7, wrow_ref.shape[0])
        wcol_ref[:, part] = one_hot(number & (LANES - 1), LANES)
    cellwi_ref[...] = cells_sum(index_ref, row_ref, col_ref, scaled_ref).reshape(cellwi_ref.shape)
    for part in parts(cell_ref.shape[1]):
        put_wells(index_ref[:, part], wrow_ref, wscaled_ref, part)
    storage_ref[...] = wells_sum(wscaled_ref, wcol_ref, storage_ref.shape[0])


def put_scaled(values, col_ref, scaled_ref, part):
    scaled_ref[0:LANES, part], scaled_ref[LANES:, part] = scaled(col_ref[:, part], values)


def cells_sum(values_ref, row_ref, col_ref, scaled_ref):
    if values_ref is not None:
        for part in parts(row_ref.shape[1]):
            put_scaled(values_ref[:, part], col_ref, scaled_ref, part)
    both = dot_nt(row_ref[...], scaled_ref[...])
    return both[:, :LANES] + both[:, LANES:]


def put_wells(values, wrow_ref, wscaled_ref, part):
    rows = wrow_ref.shape[0]
    wscaled_ref[0:rows, part], wscaled_ref[rows:, part] = scaled(wrow_ref[:, part], values)


def wells_sum(wscaled_ref, wcol_ref, wells):
    return halves_sum(dot_nt(wscaled_ref[...], wcol_ref[...]))[:wells]


def perforation_sums(direction, row_ref, col_ref, wrow_ref, wcol_ref, index_ref, wscaled_ref, wells):
    fieldt = stack_split(direction.reshape(-1, LANES).T)
    for part in parts(row_ref.shape[1]):
        values = picked_sum(col_ref[:, part], halves_sum(dot_nn(fieldt, row_ref[:, part])))
        put_wells(index_ref[:, part] * values, wrow_ref, wscaled_ref, part)
    return wells_sum(wscaled_ref, wcol_ref, wells)


def start_kernel(
    right_ref, lateral_ref, accumulation_ref, cellwi_ref, zlow_ref, zup_ref,
    ilow_ref, iup_ref, xlow_ref, xup_ref, row_ref, col_ref, wrow_ref, wcol_ref, index_ref,
    til_ref, tiu_ref, txl_ref, txu_ref, diagonal_ref, inverse_ref, direction_ref, sums_ref, wscaled_ref,
    *, scale,
):
    lateral = lateral_ref[...]
    gi, gx = lax.axis_index("inline"), lax.axis_index("xline")
    low, up = neighbours(
        lateral,
        jnp.where(gi == 0, 0.0, ilow_ref[...]),
        jnp.where(gi == lax.axis_size("inline") - 1, 0.0, iup_ref[...]),
        0,
    )
    til, tiu = harmonic_average(lateral, low), harmonic_average(lateral, up)
    low, up = neighbours(
        lateral,
        jnp.where(gx == 0, 0.0, xlow_ref[...]),
        jnp.where(gx == lax.axis_size("xline") - 1, 0.0, xup_ref[...]),
        1,
    )
    txl, txu = harmonic_average(lateral, low), harmonic_average(lateral, up)
    til_ref[...], tiu_ref[...], txl_ref[...], txu_ref[...] = til, tiu, txl, txu
    diagonal = accumulation_ref[...] + til + tiu + txl + txu + zlow_ref[...] + zup_ref[...] + cellwi_ref[...]
    inverse = 1.0 / diagonal
    direction = right_ref[...] * inverse * scale
    diagonal_ref[...] = diagonal
    inverse_ref[...] = inverse
    direction_ref[...] = direction
    sums_ref[...] = perforation_sums(direction, row_ref, col_ref, wrow_ref, wcol_ref, index_ref, wscaled_ref, sums_ref.shape[0])


def sweep_kernel(
    residual_ref, direction_ref, pressure_ref, diagonal_ref, inverse_ref,
    til_ref, tiu_ref, txl_ref, txu_ref, zlow_ref, zup_ref,
    ilow_ref, iup_ref, xlow_ref, xup_ref, sums_ref, storage_ref,
    row_ref, col_ref, wrow_ref, wcol_ref, index_ref,
    *rest, keep, gain, first,
):
    last = keep is None
    if last:
        next_pressure_ref, next_residual_ref, scaled_ref = rest
    else:
        next_pressure_ref, next_residual_ref, next_direction_ref, next_sums_ref, scaled_ref, wscaled_ref = rest
    wells = sums_ref.shape[0]
    bottom = sums_ref[...] / (1.0 + storage_ref[...])
    spare = wrow_ref.shape[0] - wells
    if spare:
        bottom = jnp.concatenate([bottom, jnp.zeros((spare, LANES), jnp.float32)], axis=0)
    table = stack_split(bottom)
    for part in parts(row_ref.shape[1]):
        values = picked_sum(wrow_ref[:, part], halves_sum(dot_nn(table, wcol_ref[:, part])))
        put_scaled(index_ref[:, part] * values, col_ref, scaled_ref, part)
    direction = direction_ref[...]
    ilow, iup = neighbours(direction, ilow_ref[...], iup_ref[...], 0)
    xlow, xup = neighbours(direction, xlow_ref[...], xup_ref[...], 1)
    below, above = layers(direction)
    beside = (
        til_ref[...] * ilow + tiu_ref[...] * iup + txl_ref[...] * xlow + txu_ref[...] * xup
        + zlow_ref[...] * below + zup_ref[...] * above
    )
    wells_term = cells_sum(None, row_ref, col_ref, scaled_ref).reshape(direction.shape)
    residual = residual_ref[...] - (diagonal_ref[...] * direction - beside - wells_term)
    next_residual_ref[...] = residual
    if first:
        next_pressure_ref[...] = direction
    else:
        next_pressure_ref[...] = pressure_ref[...] + direction
    if not last:
        following = keep * direction + gain * (residual * inverse_ref[...])
        next_direction_ref[...] = following
        next_sums_ref[...] = perforation_sums(
            following, row_ref, col_ref, wrow_ref, wcol_ref, index_ref, wscaled_ref, wells
        )


def body(
    right_side,
    facies,
    facies_table,
    thickness,
    accumulation,
    perforation_cell,
    perf_owner,
    perf_well,
    perf_index,
):
    shape = right_side.shape
    f32 = jnp.float32
    grid = jax.ShapeDtypeStruct(shape, f32)
    n_perf = perforation_cell.shape[0]
    n_dev = lax.axis_size("inline") * lax.axis_size("xline")
    wells = -(-n_dev * WELL_DEV // (8 * LANES)) * 8
    wells_hot = -(-wells // 16) * 16
    sums = jax.ShapeDtypeStruct((wells, LANES), f32)
    faces = [jax.ShapeDtypeStruct((size, LANES), f32) for size in (shape[1], shape[1], shape[0], shape[0])]
    cell = perforation_cell.reshape(1, n_perf)
    owner = perf_owner.reshape(1, n_perf)
    well = perf_well.reshape(1, n_perf)
    index = perf_index.reshape(1, n_perf)
    rows = shape[0] * shape[1]
    hots = tuple(jax.ShapeDtypeStruct((size, n_perf), jnp.bfloat16) for size in (rows, LANES, wells_hot, LANES))
    scaled_scratch = pltpu.VMEM((2 * LANES, n_perf), jnp.bfloat16)
    wscaled_scratch = pltpu.VMEM((2 * wells_hot, n_perf), jnp.bfloat16)

    row_i32 = jax.ShapeDtypeStruct((1, n_perf), jnp.int32)
    row_f32 = jax.ShapeDtypeStruct((1, n_perf), f32)
    ia, ib, xa, xb, lateral, vertical, right_side, accumulation, cell, number, index = pl.pallas_call(
        load_kernel,
        out_shape=(*faces, grid, grid, grid, grid, row_i32, row_i32, row_f32),
        in_specs=[HBM] * 9,
        out_specs=(VMEM,) * 11,
        scratch_shapes=[
            pltpu.SMEM(facies_table.shape, f32),
            pltpu.VMEM(shape, jnp.int32),
            pltpu.VMEM(shape, f32),
            pltpu.VMEM((1, n_perf), jnp.int32),
            pltpu.VMEM((1, n_perf), jnp.int32),
            pltpu.SemaphoreType.DMA((9,)),
        ],
        compiler_params=SMALL,
    )(*(
        pltpu.with_memory_space_constraint(value, pltpu.HBM)
        for value in (facies_table, facies, thickness, right_side, accumulation, cell, owner, well, index)
    ))
    lateral_halo = side_exchange({"inline": (ia, ib), "xline": (xa, xb)})
    cellwi, storage, zlow, zup, *hot = pl.pallas_call(
        perforation_kernel,
        out_shape=(grid, sums, grid, grid, *hots),
        in_specs=[VMEM] * 4,
        out_specs=(VMEM,) * 8,
        scratch_shapes=[scaled_scratch, wscaled_scratch],
        compiler_params=PARAMS,
    )(vertical, cell, number, index)

    theta = (HIGH_BOUND + LOW_BOUND) / 2.0
    delta = (HIGH_BOUND - LOW_BOUND) / 2.0
    sigma = theta / delta
    rho_now = 1.0 / sigma
    til, tiu, txl, txu, diagonal, inverse, direction, partial = pl.pallas_call(
        functools.partial(start_kernel, scale=1.0 / theta),
        out_shape=(grid,) * 7 + (sums,),
        in_specs=[VMEM] * 15,
        out_specs=(VMEM,) * 8,
        scratch_shapes=[wscaled_scratch],
        compiler_params=PARAMS,
    )(right_side, lateral, accumulation, cellwi, zlow, zup,
      *lateral_halo["inline"], *lateral_halo["xline"], *hot, index)

    residual, pressure = right_side, right_side
    for sweep in range(SWEEPS):
        last = sweep + 1 == SWEEPS
        if sweep == 0:
            (total, storage), halo = all_sum((partial, storage), all_sides(direction))
        else:
            total, halo = all_sum(partial, all_sides(direction))
        keep = gain = None
        if not last:
            rho_next = 1.0 / (2.0 * sigma - rho_now)
            keep, gain = rho_next * rho_now, 2.0 * rho_next / delta
            rho_now = rho_next
        results = pl.pallas_call(
            functools.partial(sweep_kernel, keep=keep, gain=gain, first=sweep == 0),
            out_shape=(grid, grid) if last else (grid, grid, grid, sums),
            in_specs=[VMEM] * 22,
            out_specs=(VMEM,) * (2 if last else 4),
            scratch_shapes=[scaled_scratch] if last else [scaled_scratch, wscaled_scratch],
            compiler_params=PARAMS,
        )(residual, direction, pressure, diagonal, inverse, til, tiu, txl, txu, zlow, zup,
          *halo["inline"], *halo["xline"], total, storage, *hot, index)
        if last:
            pressure, residual = results
        else:
            pressure, residual, direction, partial = results
    return pressure, residual


def solution(mesh):
    in_specs = (
        P("inline", "xline", None),
        P("inline", "xline", None),
        P(),
        P("inline", "xline", None),
        P("inline", "xline", None),
        P(("inline", "xline")),
        P(("inline", "xline"), None),
        P(("inline", "xline")),
        P(("inline", "xline")),
    )
    out_specs = (P("inline", "xline", None), P("inline", "xline", None))
    return jax.shard_map(body, mesh=mesh, in_specs=in_specs, out_specs=out_specs, check_vma=False)
```

```python
import functools

import jax
import jax.numpy as jnp
from jax import lax
from jax.experimental import pallas as pl
from jax.experimental.pallas import tpu as pltpu
from jax.sharding import PartitionSpec as P

SWEEPS = 3
WELL_DEV = 160
LANES = 128
LOW_BOUND = 0.1
HIGH_BOUND = 2.0
CHUNK = 512
MESH_AXES = ("inline", "xline")

VMEM = pl.BlockSpec(memory_space=pltpu.VMEM)
HBM = pl.BlockSpec(memory_space=pltpu.HBM)
PARAMS = pltpu.CompilerParams(vmem_limit_bytes=16 * 1024 * 1024)
SMALL = pltpu.CompilerParams(vmem_limit_bytes=4 * 1024 * 1024)


def pair_permute(value, partner):
    ni, nx = lax.axis_size("inline"), lax.axis_size("xline")
    pairs = []
    for i in range(ni):
        for j in range(nx):
            i2, j2 = partner(i, j)
            pairs.append((i * nx + j, i2 * nx + j2))
    return lax.ppermute(value, MESH_AXES, pairs)


def xor_permute(value, inline_mask, xline_mask):
    return pair_permute(value, lambda i, j: (i ^ inline_mask, j ^ xline_mask))


def bits_of(count):
    bits = count.bit_length() - 1
    if 1 << bits != count:
        raise ValueError("axis size")
    return bits


def side_masks(count):
    return [(2 << s) - 1 for s in range(bits_of(count))]


def stages_of(count):
    bits = bits_of(count)
    cuts = ([1] if bits % 2 else []) + [2] * (bits // 2)
    stages, low = [], 0
    for width in cuts:
        stages.append([pattern << low | (1 << low) - 1 for pattern in range(1, 1 << width)])
        low += width
    return stages


def all_stages():
    return [[(0, mask) for mask in masks] for masks in stages_of(lax.axis_size("xline"))] + [
        [(mask, 1) for mask in masks] for masks in stages_of(lax.axis_size("inline"))
    ]


SPLIT_STAGES = [[(0, 1)], [(0, 3), (0, 4), (0, 7)], [(1, 0), (2, 1), (3, 1)]]


def two_kinds():
    return [len(stage) for stage in all_stages()] == [len(stage) for stage in SPLIT_STAGES]


def exchange_stage(value, stage, riders, arrived):
    rows = value.shape[0]
    total = value
    for masks in stage:
        rider = riders.get(masks)
        if rider is None:
            got = xor_permute(value, *masks)
        else:
            got = xor_permute(jnp.concatenate([value, rider], axis=0), *masks)
            arrived[masks] = got[rows:]
        total = total + got[:rows]
    return total


def all_sum(message, far, rows, kind=None):
    ni, nx = lax.axis_size("inline"), lax.axis_size("xline")
    lines = far.shape[0]
    first, *others = all_stages()
    if kind is not None:
        others = SPLIT_STAGES[1:]
    got = xor_permute(message, 0, 1)
    value = message[:rows] + got[:rows]
    own = jnp.split(message[rows + lines :], 2, axis=0)
    mate = jnp.split(got[rows + lines :], 2, axis=0)
    arrived = {(0, 1): got[rows : rows + lines]}
    riders = {(0, mask): far for mask in side_masks(nx)[1:]}
    for stage in others:
        for mask, flip in stage:
            if mask in side_masks(ni):
                riders[mask, flip] = (mate if flip else own)[0 if mask == 1 else 1]
    value = exchange_more(value, message[:rows], first, riders, arrived)
    if kind is not None:
        half = rows // 2
        value = jnp.where(kind == 0, value[:half], value[half:])
    for stage in others:
        value = exchange_stage(value, stage, riders, arrived)
    if kind is not None:
        swapped = xor_permute(value, 0, 1)
        value = jnp.concatenate(
            [jnp.where(kind == 0, value, swapped), jnp.where(kind == 0, swapped, value)], axis=0
        )
    beside = {masks[0] or -masks[1]: face for masks, face in arrived.items()}
    return (
        value,
        [beside[mask] for mask in side_masks(ni)],
        [beside[-mask] for mask in side_masks(nx)],
    )


def exchange_more(value, own, first, riders, arrived):
    rows = own.shape[0]
    for masks in first[1:]:
        rider = riders.get(masks)
        got = xor_permute(own if rider is None else jnp.concatenate([own, rider], axis=0), *masks)
        if rider is not None:
            arrived[masks] = got[rows:]
        value = value + got[:rows]
    return value


def beyond(index, count):
    other = index - 1 if index % 2 == 0 else index + 1
    return other if 0 <= other < count else None


def side_exchange(ia, ib, xa, xb):
    ni, nx = lax.axis_size("inline"), lax.axis_size("xline")

    def inline_far(i, j):
        other = beyond(i, ni)
        return (i, j ^ 1) if other is None else (other, j)

    def xline_far(i, j):
        other = beyond(j, nx)
        return (i ^ 1, j) if other is None else (i, other)

    return (
        xor_permute(ia, 1, 0), pair_permute(ib, inline_far),
        xor_permute(xa, 0, 1), pair_permute(xb, xline_far),
    )


def harmonic_average(first, second):
    return 2.0 * first * second / (first + second)


def split2(value):
    high = value.astype(jnp.bfloat16)
    low = (value - high.astype(jnp.float32)).astype(jnp.bfloat16)
    return high, low


def stack_split(value):
    return jnp.concatenate(split2(value), axis=0)


def dot_nt(a, b):
    return lax.dot_general(a, b, (((1,), (1,)), ((), ())), preferred_element_type=jnp.float32)


def dot_nn(a, b):
    return lax.dot_general(a, b, (((1,), (0,)), ((), ())), preferred_element_type=jnp.float32)


def halves_sum(both):
    half = both.shape[0] // 2
    return both[:half] + both[half:]


def one_hot(index_row, rows):
    shape = (rows, index_row.shape[1])
    hit = lax.broadcasted_iota(jnp.int32, shape, 0) == index_row
    return jnp.where(hit, 1.0, 0.0).astype(jnp.bfloat16)


def scaled(hot, values):
    rows, count = hot.shape
    tiles = hot.reshape(rows // 16, 16, count)
    pieces = split2(jnp.broadcast_to(values, (16, count)))
    return [(tiles * piece[None]).reshape(rows, count) for piece in pieces]


def picked_sum(hot, values):
    return jnp.sum(hot.astype(jnp.float32) * values, axis=0, keepdims=True)


def parts(count):
    return [pl.ds(start, CHUNK) for start in range(0, count, CHUNK)]


def lookup(facies, table_ref, row):
    result = jnp.full(facies.shape, table_ref[row, 0], jnp.float32)
    for entry in range(1, table_ref.shape[1]):
        result = jnp.where(facies == entry, table_ref[row, entry], result)
    return result


def neighbours(cells, lower, upper, dim):
    if dim == 0:
        return (
            jnp.concatenate([lower[None], cells[:-1]], axis=0),
            jnp.concatenate([cells[1:], upper[None]], axis=0),
        )
    size = cells.shape[1]
    place = lax.broadcasted_iota(jnp.int32, cells.shape, 1)
    return (
        jnp.where(place == 0, lower[:, None], pltpu.roll(cells, 1, 1)),
        jnp.where(place == size - 1, upper[:, None], pltpu.roll(cells, size - 1, 1)),
    )


def layers(cells):
    return pltpu.roll(cells, 1, 2), pltpu.roll(cells, LANES - 1, 2)


def side_faces(cells, axis):
    lower, upper = (cells[0], cells[-1]) if axis == "inline" else (cells[:, 0], cells[:, -1])
    odd = lax.axis_index(axis) % 2 == 1
    return jnp.where(odd, lower, upper), jnp.where(odd, upper, lower)


def halo(axis, faces):
    index = lax.axis_index(axis)
    even = index % 2 == 0
    apart = index ^ jnp.where(even, index - 1, index + 1)
    far = faces[-1]
    for mask, face in list(zip(side_masks(lax.axis_size(axis)), faces))[1:-1]:
        far = jnp.where(apart == mask, face, far)
    return jnp.where(even, far, faces[0]), jnp.where(even, faces[0], far)


def put_message(direction, blocks, message_ref, far_ref):
    ia, ib = side_faces(direction, "inline")
    xa, xb = side_faces(direction, "xline")
    start = 0
    for block in (*blocks, xa, ia, ib):
        message_ref[start : start + block.shape[0], :] = block
        start += block.shape[0]
    far_ref[...] = xb


def load_kernel(
    table_hbm, facies_hbm, thickness_hbm, right_hbm, accumulation_hbm, cell_hbm, owner_hbm, well_hbm, index_hbm,
    ia_ref, ib_ref, xa_ref, xb_ref, lateral_ref, vertical_ref,
    right_ref, accumulation_ref, cell_ref, number_ref, index_ref,
    table_ref, facies_ref, thickness_ref, owner_ref, well_ref, sems,
):
    copies = [
        pltpu.make_async_copy(source, target, sems.at[slot])
        for slot, (source, target) in enumerate(
            (
                (table_hbm, table_ref), (facies_hbm, facies_ref), (thickness_hbm, thickness_ref),
                (owner_hbm, owner_ref), (well_hbm, well_ref), (right_hbm, right_ref),
                (accumulation_hbm, accumulation_ref), (cell_hbm, cell_ref), (index_hbm, index_ref),
            )
        )
    ]
    for copy in copies:
        copy.start()
    for copy in copies:
        copy.wait()
    facies, thickness = facies_ref[...], thickness_ref[...]
    lateral = lookup(facies, table_ref, 0) * thickness
    lateral_ref[...] = lateral
    vertical_ref[...] = lookup(facies, table_ref, 1) / thickness
    ia_ref[...], ib_ref[...] = side_faces(lateral, "inline")
    xa_ref[...], xb_ref[...] = side_faces(lateral, "xline")
    number_ref[...] = owner_ref[...] * WELL_DEV + well_ref[...]


def perforation_kernel(
    vertical_ref, cell_ref, number_ref, index_ref,
    cellwi_ref, storage_ref, zlow_ref, zup_ref, row_ref, col_ref, wrow_ref, wcol_ref, scaled_ref, wscaled_ref,
):
    vertical = vertical_ref[...]
    below, above = layers(vertical)
    place = lax.broadcasted_iota(jnp.int32, vertical.shape, 2)
    zlow_ref[...] = jnp.where(place == 0, 0.0, harmonic_average(vertical, below))
    zup_ref[...] = jnp.where(place == LANES - 1, 0.0, harmonic_average(vertical, above))
    for part in parts(cell_ref.shape[1]):
        cell, number = cell_ref[:, part], number_ref[:, part]
        row_ref[:, part] = one_hot(cell >> 7, row_ref.shape[0])
        col_ref[:, part] = one_hot(cell & (LANES - 1), LANES)
        wrow_ref[:, part] = one_hot(number >> 7, wrow_ref.shape[0])
        wcol_ref[:, part] = one_hot(number & (LANES - 1), LANES)
    cellwi_ref[...] = cells_sum(index_ref, row_ref, col_ref, scaled_ref).reshape(cellwi_ref.shape)
    for part in parts(cell_ref.shape[1]):
        put_wells(index_ref[:, part], wrow_ref, wscaled_ref, part)
    storage_ref[...] = wells_sum(wscaled_ref, wcol_ref, storage_ref.shape[0])


def put_scaled(values, col_ref, scaled_ref, part):
    scaled_ref[0:LANES, part], scaled_ref[LANES:, part] = scaled(col_ref[:, part], values)


def cells_sum(values_ref, row_ref, col_ref, scaled_ref):
    if values_ref is not None:
        for part in parts(row_ref.shape[1]):
            put_scaled(values_ref[:, part], col_ref, scaled_ref, part)
    both = dot_nt(row_ref[...], scaled_ref[...])
    return both[:, :LANES] + both[:, LANES:]


def put_wells(values, wrow_ref, wscaled_ref, part):
    rows = wrow_ref.shape[0]
    wscaled_ref[0:rows, part], wscaled_ref[rows:, part] = scaled(wrow_ref[:, part], values)


def wells_sum(wscaled_ref, wcol_ref, wells):
    return halves_sum(dot_nt(wscaled_ref[...], wcol_ref[...]))[:wells]


def perforation_sums(direction, row_ref, col_ref, wrow_ref, wcol_ref, index_ref, wscaled_ref, wells):
    fieldt = stack_split(direction.reshape(-1, LANES).T)
    for part in parts(row_ref.shape[1]):
        values = picked_sum(col_ref[:, part], halves_sum(dot_nn(fieldt, row_ref[:, part])))
        put_wells(index_ref[:, part] * values, wrow_ref, wscaled_ref, part)
    return wells_sum(wscaled_ref, wcol_ref, wells)


def start_kernel(
    right_ref, lateral_ref, accumulation_ref, cellwi_ref, zlow_ref, zup_ref,
    ia_ref, ib_ref, xa_ref, xb_ref, storage_ref, row_ref, col_ref, wrow_ref, wcol_ref, index_ref,
    til_ref, tiu_ref, txl_ref, txu_ref, diagonal_ref, inverse_ref, direction_ref, message_ref, far_ref, kind_ref,
    wscaled_ref,
    *, scale,
):
    lateral = lateral_ref[...]
    gi, gx = lax.axis_index("inline"), lax.axis_index("xline")
    low, up = halo("inline", [ia_ref[...], ib_ref[...]])
    low = jnp.where(gi == 0, 0.0, low)
    up = jnp.where(gi == lax.axis_size("inline") - 1, 0.0, up)
    low, up = neighbours(lateral, low, up, 0)
    til, tiu = harmonic_average(lateral, low), harmonic_average(lateral, up)
    low, up = halo("xline", [xa_ref[...], xb_ref[...]])
    low = jnp.where(gx == 0, 0.0, low)
    up = jnp.where(gx == lax.axis_size("xline") - 1, 0.0, up)
    low, up = neighbours(lateral, low, up, 1)
    txl, txu = harmonic_average(lateral, low), harmonic_average(lateral, up)
    til_ref[...], tiu_ref[...], txl_ref[...], txu_ref[...] = til, tiu, txl, txu
    diagonal = accumulation_ref[...] + til + tiu + txl + txu + zlow_ref[...] + zup_ref[...] + cellwi_ref[...]
    inverse = 1.0 / diagonal
    direction = right_ref[...] * inverse * scale
    diagonal_ref[...] = diagonal
    inverse_ref[...] = inverse
    direction_ref[...] = direction
    storage = storage_ref[...]
    sums = perforation_sums(
        direction, row_ref, col_ref, wrow_ref, wcol_ref, index_ref, wscaled_ref, storage.shape[0]
    )
    put_message(direction, [sums, storage], message_ref, far_ref)
    kind_ref[...] = jnp.full(kind_ref.shape, (gx ^ (gx >> 1) ^ (gi >> 1)) & 1, jnp.int32)


def sweep_kernel(*refs, keep, gain, first, sides):
    (
        residual_ref, direction_ref, pressure_ref, diagonal_ref, inverse_ref,
        til_ref, tiu_ref, txl_ref, txu_ref, zlow_ref, zup_ref,
    ) = refs[:11]
    inline_faces = [ref[...] for ref in refs[11 : 11 + sides[0]]]
    xline_faces = [ref[...] for ref in refs[11 + sides[0] : 11 + sum(sides)]]
    sums_ref, storage_ref, row_ref, col_ref, wrow_ref, wcol_ref, index_ref, *rest = refs[11 + sum(sides) :]
    last = keep is None
    if last:
        next_pressure_ref, next_residual_ref, scaled_ref = rest
    else:
        (
            next_pressure_ref, next_residual_ref, next_direction_ref, message_ref, far_ref,
            scaled_ref, wscaled_ref,
        ) = rest
    wells = sums_ref.shape[0]
    bottom = sums_ref[...] / (1.0 + storage_ref[...])
    spare = wrow_ref.shape[0] - wells
    if spare:
        bottom = jnp.concatenate([bottom, jnp.zeros((spare, LANES), jnp.float32)], axis=0)
    table = stack_split(bottom)
    for part in parts(row_ref.shape[1]):
        values = picked_sum(wrow_ref[:, part], halves_sum(dot_nn(table, wcol_ref[:, part])))
        put_scaled(index_ref[:, part] * values, col_ref, scaled_ref, part)
    direction = direction_ref[...]
    ilow, iup = neighbours(direction, *halo("inline", inline_faces), 0)
    xlow, xup = neighbours(direction, *halo("xline", xline_faces), 1)
    below, above = layers(direction)
    beside = (
        til_ref[...] * ilow + tiu_ref[...] * iup + txl_ref[...] * xlow + txu_ref[...] * xup
        + zlow_ref[...] * below + zup_ref[...] * above
    )
    wells_term = cells_sum(None, row_ref, col_ref, scaled_ref).reshape(direction.shape)
    residual = residual_ref[...] - (diagonal_ref[...] * direction - beside - wells_term)
    next_residual_ref[...] = residual
    if first:
        next_pressure_ref[...] = direction
    else:
        next_pressure_ref[...] = pressure_ref[...] + direction
    if not last:
        following = keep * direction + gain * (residual * inverse_ref[...])
        next_direction_ref[...] = following
        next_sums = perforation_sums(
            following, row_ref, col_ref, wrow_ref, wcol_ref, index_ref, wscaled_ref, wells
        )
        put_message(following, [next_sums], message_ref, far_ref)


def body(
    right_side,
    facies,
    facies_table,
    thickness,
    accumulation,
    perforation_cell,
    perf_owner,
    perf_well,
    perf_index,
):
    shape = right_side.shape
    f32 = jnp.float32
    grid = jax.ShapeDtypeStruct(shape, f32)
    n_perf = perforation_cell.shape[0]
    n_dev = lax.axis_size("inline") * lax.axis_size("xline")
    wells = -(-n_dev * WELL_DEV // (8 * LANES)) * 8
    wells_hot = -(-wells // 16) * 16
    sums = jax.ShapeDtypeStruct((wells, LANES), f32)
    faces = [jax.ShapeDtypeStruct((size, LANES), f32) for size in (shape[1], shape[1], shape[0], shape[0])]
    cell = perforation_cell.reshape(1, n_perf)
    owner = perf_owner.reshape(1, n_perf)
    well = perf_well.reshape(1, n_perf)
    index = perf_index.reshape(1, n_perf)
    rows = shape[0] * shape[1]
    hots = tuple(jax.ShapeDtypeStruct((size, n_perf), jnp.bfloat16) for size in (rows, LANES, wells_hot, LANES))
    scaled_scratch = pltpu.VMEM((2 * LANES, n_perf), jnp.bfloat16)
    wscaled_scratch = pltpu.VMEM((2 * wells_hot, n_perf), jnp.bfloat16)

    row_i32 = jax.ShapeDtypeStruct((1, n_perf), jnp.int32)
    row_f32 = jax.ShapeDtypeStruct((1, n_perf), f32)
    ia, ib, xa, xb, lateral, vertical, right_side, accumulation, cell, number, index = pl.pallas_call(
        load_kernel,
        out_shape=(*faces, grid, grid, grid, grid, row_i32, row_i32, row_f32),
        in_specs=[HBM] * 9,
        out_specs=(VMEM,) * 11,
        scratch_shapes=[
            pltpu.SMEM(facies_table.shape, f32),
            pltpu.VMEM(shape, jnp.int32),
            pltpu.VMEM(shape, f32),
            pltpu.VMEM((1, n_perf), jnp.int32),
            pltpu.VMEM((1, n_perf), jnp.int32),
            pltpu.SemaphoreType.DMA((9,)),
        ],
        compiler_params=SMALL,
    )(*(
        pltpu.with_memory_space_constraint(value, pltpu.HBM)
        for value in (facies_table, facies, thickness, right_side, accumulation, cell, owner, well, index)
    ))
    lateral_faces = side_exchange(ia, ib, xa, xb)
    cellwi, storage, zlow, zup, *hot = pl.pallas_call(
        perforation_kernel,
        out_shape=(grid, sums, grid, grid, *hots),
        in_specs=[VMEM] * 4,
        out_specs=(VMEM,) * 8,
        scratch_shapes=[scaled_scratch, wscaled_scratch],
        compiler_params=PARAMS,
    )(vertical, cell, number, index)

    theta = (HIGH_BOUND + LOW_BOUND) / 2.0
    delta = (HIGH_BOUND - LOW_BOUND) / 2.0
    sigma = theta / delta
    rho_now = 1.0 / sigma
    face_rows = shape[0] + 2 * shape[1]
    start_message = jax.ShapeDtypeStruct((2 * wells + face_rows, LANES), f32)
    sweep_message = jax.ShapeDtypeStruct((wells + face_rows, LANES), f32)
    kinds = jax.ShapeDtypeStruct((wells, LANES), jnp.int32)
    til, tiu, txl, txu, diagonal, inverse, direction, message, far, kind = pl.pallas_call(
        functools.partial(start_kernel, scale=1.0 / theta),
        out_shape=(grid,) * 7 + (start_message, faces[2], kinds),
        in_specs=[VMEM] * 16,
        out_specs=(VMEM,) * 10,
        scratch_shapes=[wscaled_scratch],
        compiler_params=PARAMS,
    )(right_side, lateral, accumulation, cellwi, zlow, zup, *lateral_faces, storage, *hot, index)

    residual, pressure = right_side, right_side
    for sweep in range(SWEEPS):
        last = sweep + 1 == SWEEPS
        if sweep == 0:
            both, inline_faces, xline_faces = all_sum(message, far, 2 * wells, kind if two_kinds() else None)
            total, storage = both[:wells], both[wells:]
        else:
            total, inline_faces, xline_faces = all_sum(message, far, wells)
        keep = gain = None
        if not last:
            rho_next = 1.0 / (2.0 * sigma - rho_now)
            keep, gain = rho_next * rho_now, 2.0 * rho_next / delta
            rho_now = rho_next
        sides = (len(inline_faces), len(xline_faces))
        results = pl.pallas_call(
            functools.partial(sweep_kernel, keep=keep, gain=gain, first=sweep == 0, sides=sides),
            out_shape=(grid, grid) if last else (grid, grid, grid, sweep_message, faces[2]),
            in_specs=[VMEM] * (18 + sum(sides)),
            out_specs=(VMEM,) * (2 if last else 5),
            scratch_shapes=[scaled_scratch] if last else [scaled_scratch, wscaled_scratch],
            compiler_params=PARAMS,
        )(residual, direction, pressure, diagonal, inverse, til, tiu, txl, txu, zlow, zup,
          *inline_faces, *xline_faces, total, storage, *hot, index)
        if last:
            pressure, residual = results
        else:
            pressure, residual, direction, message, far = results
    return pressure, residual


def solution(mesh):
    in_specs = (
        P("inline", "xline", None),
        P("inline", "xline", None),
        P(),
        P("inline", "xline", None),
        P("inline", "xline", None),
        P(("inline", "xline")),
        P(("inline", "xline"), None),
        P(("inline", "xline")),
        P(("inline", "xline")),
    )
    out_specs = (P("inline", "xline", None), P("inline", "xline", None))
    return jax.shard_map(body, mesh=mesh, in_specs=in_specs, out_specs=out_specs, check_vma=False)
```

```python
import functools

import jax
import jax.numpy as jnp
from jax import lax
from jax.experimental import pallas as pl
from jax.experimental.pallas import tpu as pltpu
from jax.sharding import PartitionSpec as P

SWEEPS = 3
WELL_DEV = 160
LANES = 128
LOW_BOUND = 0.1
HIGH_BOUND = 2.0
CHUNK = 512
MESH_AXES = ("inline", "xline")

VMEM = pl.BlockSpec(memory_space=pltpu.VMEM)
HBM = pl.BlockSpec(memory_space=pltpu.HBM)
PARAMS = pltpu.CompilerParams(vmem_limit_bytes=16 * 1024 * 1024)
SMALL = pltpu.CompilerParams(vmem_limit_bytes=4 * 1024 * 1024)


def pair_permute(value, partner):
    ni, nx = lax.axis_size("inline"), lax.axis_size("xline")
    pairs = []
    for i in range(ni):
        for j in range(nx):
            i2, j2 = partner(i, j)
            pairs.append((i * nx + j, i2 * nx + j2))
    return lax.ppermute(value, MESH_AXES, pairs)


def xor_permute(value, inline_mask, xline_mask):
    return pair_permute(value, lambda i, j: (i ^ inline_mask, j ^ xline_mask))


def bits_of(count):
    bits = count.bit_length() - 1
    if 1 << bits != count:
        raise ValueError("axis size")
    return bits


def side_masks(count):
    return [(2 << s) - 1 for s in range(bits_of(count))]


def stages_of(count):
    bits = bits_of(count)
    cuts = ([1] if bits % 2 else []) + [2] * (bits // 2)
    stages, low = [], 0
    for width in cuts:
        stages.append([pattern << low | (1 << low) - 1 for pattern in range(1, 1 << width)])
        low += width
    return stages


def all_stages():
    return [[(0, mask) for mask in masks] for masks in stages_of(lax.axis_size("xline"))] + [
        [(mask, 1) for mask in masks] for masks in stages_of(lax.axis_size("inline"))
    ]


SPLIT_STAGES = [[(0, 1)], [(0, 3), (0, 4), (0, 7)], [(1, 0), (2, 1), (3, 1)]]


def two_kinds():
    return [len(stage) for stage in all_stages()] == [len(stage) for stage in SPLIT_STAGES]


def exchange_stage(value, stage, riders, arrived):
    rows = value.shape[0]
    total = value
    for masks in stage:
        rider = riders.get(masks)
        if rider is None:
            got = xor_permute(value, *masks)
        else:
            got = xor_permute(jnp.concatenate([value, rider], axis=0), *masks)
            arrived[masks] = got[rows:]
        total = total + got[:rows]
    return total


def all_sum(message, far, rows, kind=None):
    ni, nx = lax.axis_size("inline"), lax.axis_size("xline")
    lines = far.shape[0]
    first, *others = all_stages()
    if kind is not None:
        others = SPLIT_STAGES[1:]
    got = xor_permute(message, 0, 1)
    value = message[:rows] + got[:rows]
    own = jnp.split(message[rows + lines :], 2, axis=0)
    mate = jnp.split(got[rows + lines :], 2, axis=0)
    arrived = {(0, 1): got[rows : rows + lines]}
    riders = {(0, mask): far for mask in range(2, nx)}
    for stage in others:
        for mask, flip in stage:
            if mask in side_masks(ni):
                riders[mask, flip] = (mate if flip else own)[0 if mask == 1 else 1]
    value = exchange_more(value, message[:rows], first, riders, arrived)
    if kind is not None:
        half = rows // 2
        value = jnp.where(kind == 0, value[:half], value[half:])
    for stage in others:
        value = exchange_stage(value, stage, riders, arrived)
    if kind is not None:
        swapped = xor_permute(value, 0, 1)
        value = jnp.concatenate(
            [jnp.where(kind == 0, value, swapped), jnp.where(kind == 0, swapped, value)], axis=0
        )
    beside = {masks[0] or -masks[1]: face for masks, face in arrived.items()}
    return (
        value,
        [beside[mask] for mask in side_masks(ni)],
        [beside[-mask] for mask in side_masks(nx)],
    )


def exchange_more(value, own, first, riders, arrived):
    rows = own.shape[0]
    for masks in first[1:]:
        rider = riders.get(masks)
        got = xor_permute(own if rider is None else jnp.concatenate([own, rider], axis=0), *masks)
        if rider is not None:
            arrived[masks] = got[rows:]
        value = value + got[:rows]
    return value


def beyond(index, count):
    other = index - 1 if index % 2 == 0 else index + 1
    return other if 0 <= other < count else None


def side_exchange(ia, ib, xa, xb):
    ni, nx = lax.axis_size("inline"), lax.axis_size("xline")

    def inline_far(i, j):
        other = beyond(i, ni)
        return (i, j ^ 1) if other is None else (other, j)

    def xline_far(i, j):
        other = beyond(j, nx)
        return (i ^ 1, j) if other is None else (i, other)

    return (
        xor_permute(ia, 1, 0), pair_permute(ib, inline_far),
        xor_permute(xa, 0, 1), pair_permute(xb, xline_far),
    )


def harmonic_average(first, second):
    return 2.0 * first * second / (first + second)


def split2(value):
    high = value.astype(jnp.bfloat16)
    low = (value - high.astype(jnp.float32)).astype(jnp.bfloat16)
    return high, low


def stack_split(value):
    return jnp.concatenate(split2(value), axis=0)


def dot_nt(a, b):
    return lax.dot_general(a, b, (((1,), (1,)), ((), ())), preferred_element_type=jnp.float32)


def dot_nn(a, b):
    return lax.dot_general(a, b, (((1,), (0,)), ((), ())), preferred_element_type=jnp.float32)


def halves_sum(both):
    half = both.shape[0] // 2
    return both[:half] + both[half:]


def one_hot(index_row, rows):
    shape = (rows, index_row.shape[1])
    hit = lax.broadcasted_iota(jnp.int32, shape, 0) == index_row
    return jnp.where(hit, 1.0, 0.0).astype(jnp.bfloat16)


def scaled(hot, values):
    rows, count = hot.shape
    tiles = hot.reshape(rows // 16, 16, count)
    pieces = split2(jnp.broadcast_to(values, (16, count)))
    return [(tiles * piece[None]).reshape(rows, count) for piece in pieces]


def picked_sum(hot, values):
    return jnp.sum(hot.astype(jnp.float32) * values, axis=0, keepdims=True)


def parts(count):
    return [pl.ds(start, CHUNK) for start in range(0, count, CHUNK)]


def lookup(facies, table_ref, row):
    result = jnp.full(facies.shape, table_ref[row, 0], jnp.float32)
    for entry in range(1, table_ref.shape[1]):
        result = jnp.where(facies == entry, table_ref[row, entry], result)
    return result


def neighbours(cells, lower, upper, dim):
    if dim == 0:
        return (
            jnp.concatenate([lower[None], cells[:-1]], axis=0),
            jnp.concatenate([cells[1:], upper[None]], axis=0),
        )
    size = cells.shape[1]
    place = lax.broadcasted_iota(jnp.int32, cells.shape, 1)
    return (
        jnp.where(place == 0, lower[:, None], pltpu.roll(cells, 1, 1)),
        jnp.where(place == size - 1, upper[:, None], pltpu.roll(cells, size - 1, 1)),
    )


def layers(cells):
    return pltpu.roll(cells, 1, 2), pltpu.roll(cells, LANES - 1, 2)


def side_faces(cells, axis):
    lower, upper = (cells[0], cells[-1]) if axis == "inline" else (cells[:, 0], cells[:, -1])
    odd = lax.axis_index(axis) % 2 == 1
    return jnp.where(odd, lower, upper), jnp.where(odd, upper, lower)


def halo(axis, faces):
    index = lax.axis_index(axis)
    even = index % 2 == 0
    apart = index ^ jnp.where(even, index - 1, index + 1)
    far = faces[-1]
    for mask, face in list(zip(side_masks(lax.axis_size(axis)), faces))[1:-1]:
        far = jnp.where(apart == mask, face, far)
    return jnp.where(even, far, faces[0]), jnp.where(even, faces[0], far)


def put_message(direction, blocks, message_ref, far_ref):
    ia, ib = side_faces(direction, "inline")
    xa, xb = side_faces(direction, "xline")
    start = 0
    for block in (*blocks, xa, ia, ib):
        message_ref[start : start + block.shape[0], :] = block
        start += block.shape[0]
    far_ref[...] = xb


def load_kernel(
    table_hbm, facies_hbm, thickness_hbm, right_hbm, accumulation_hbm, cell_hbm, owner_hbm, well_hbm, index_hbm,
    ia_ref, ib_ref, xa_ref, xb_ref, lateral_ref, vertical_ref,
    right_ref, accumulation_ref, cell_ref, number_ref, index_ref,
    table_ref, facies_ref, thickness_ref, owner_ref, well_ref, sems,
):
    copies = [
        pltpu.make_async_copy(source, target, sems.at[slot])
        for slot, (source, target) in enumerate(
            (
                (table_hbm, table_ref), (facies_hbm, facies_ref), (thickness_hbm, thickness_ref),
                (owner_hbm, owner_ref), (well_hbm, well_ref), (right_hbm, right_ref),
                (accumulation_hbm, accumulation_ref), (cell_hbm, cell_ref), (index_hbm, index_ref),
            )
        )
    ]
    for copy in copies:
        copy.start()
    for copy in copies:
        copy.wait()
    facies, thickness = facies_ref[...], thickness_ref[...]
    lateral = lookup(facies, table_ref, 0) * thickness
    lateral_ref[...] = lateral
    vertical_ref[...] = lookup(facies, table_ref, 1) / thickness
    ia_ref[...], ib_ref[...] = side_faces(lateral, "inline")
    xa_ref[...], xb_ref[...] = side_faces(lateral, "xline")
    number_ref[...] = owner_ref[...] * WELL_DEV + well_ref[...]


def perforation_kernel(
    vertical_ref, cell_ref, number_ref, index_ref, face_ref,
    cellwi_ref, storage_ref, zlow_ref, zup_ref, row_ref, col_ref, wrow_ref, wcol_ref, face_out_ref,
    scaled_ref, wscaled_ref,
):
    face_out_ref[...] = face_ref[...]
    vertical = vertical_ref[...]
    below, above = layers(vertical)
    place = lax.broadcasted_iota(jnp.int32, vertical.shape, 2)
    zlow_ref[...] = jnp.where(place == 0, 0.0, harmonic_average(vertical, below))
    zup_ref[...] = jnp.where(place == LANES - 1, 0.0, harmonic_average(vertical, above))
    for part in parts(cell_ref.shape[1]):
        cell, number = cell_ref[:, part], number_ref[:, part]
        row_ref[:, part] = one_hot(cell >> 7, row_ref.shape[0])
        col_ref[:, part] = one_hot(cell & (LANES - 1), LANES)
        wrow_ref[:, part] = one_hot(number >> 7, wrow_ref.shape[0])
        wcol_ref[:, part] = one_hot(number & (LANES - 1), LANES)
    cellwi_ref[...] = cells_sum(index_ref, row_ref, col_ref, scaled_ref).reshape(cellwi_ref.shape)
    for part in parts(cell_ref.shape[1]):
        put_wells(index_ref[:, part], wrow_ref, wscaled_ref, part)
    storage_ref[...] = wells_sum(wscaled_ref, wcol_ref, storage_ref.shape[0])


def put_scaled(values, col_ref, scaled_ref, part):
    scaled_ref[0:LANES, part], scaled_ref[LANES:, part] = scaled(col_ref[:, part], values)


def cells_sum(values_ref, row_ref, col_ref, scaled_ref):
    if values_ref is not None:
        for part in parts(row_ref.shape[1]):
            put_scaled(values_ref[:, part], col_ref, scaled_ref, part)
    both = dot_nt(row_ref[...], scaled_ref[...])
    return both[:, :LANES] + both[:, LANES:]


def put_wells(values, wrow_ref, wscaled_ref, part):
    rows = wrow_ref.shape[0]
    wscaled_ref[0:rows, part], wscaled_ref[rows:, part] = scaled(wrow_ref[:, part], values)


def wells_sum(wscaled_ref, wcol_ref, wells):
    return halves_sum(dot_nt(wscaled_ref[...], wcol_ref[...]))[:wells]


def perforation_sums(direction, row_ref, col_ref, wrow_ref, wcol_ref, index_ref, wscaled_ref, wells):
    fieldt = stack_split(direction.reshape(-1, LANES).T)
    for part in parts(row_ref.shape[1]):
        values = picked_sum(col_ref[:, part], halves_sum(dot_nn(fieldt, row_ref[:, part])))
        put_wells(index_ref[:, part] * values, wrow_ref, wscaled_ref, part)
    return wells_sum(wscaled_ref, wcol_ref, wells)


def start_kernel(
    right_ref, lateral_ref, accumulation_ref, cellwi_ref, zlow_ref, zup_ref,
    ia_ref, ib_ref, xa_ref, xb_ref, storage_ref, row_ref, col_ref, wrow_ref, wcol_ref, index_ref,
    til_ref, tiu_ref, txl_ref, txu_ref, diagonal_ref, inverse_ref, direction_ref, message_ref, far_ref, kind_ref,
    wscaled_ref,
    *, scale,
):
    lateral = lateral_ref[...]
    gi, gx = lax.axis_index("inline"), lax.axis_index("xline")
    low, up = halo("inline", [ia_ref[...], ib_ref[...]])
    low = jnp.where(gi == 0, 0.0, low)
    up = jnp.where(gi == lax.axis_size("inline") - 1, 0.0, up)
    low, up = neighbours(lateral, low, up, 0)
    til, tiu = harmonic_average(lateral, low), harmonic_average(lateral, up)
    low, up = halo("xline", [xa_ref[...], xb_ref[...]])
    low = jnp.where(gx == 0, 0.0, low)
    up = jnp.where(gx == lax.axis_size("xline") - 1, 0.0, up)
    low, up = neighbours(lateral, low, up, 1)
    txl, txu = harmonic_average(lateral, low), harmonic_average(lateral, up)
    til_ref[...], tiu_ref[...], txl_ref[...], txu_ref[...] = til, tiu, txl, txu
    diagonal = accumulation_ref[...] + til + tiu + txl + txu + zlow_ref[...] + zup_ref[...] + cellwi_ref[...]
    inverse = 1.0 / diagonal
    direction = right_ref[...] * inverse * scale
    diagonal_ref[...] = diagonal
    inverse_ref[...] = inverse
    direction_ref[...] = direction
    storage = storage_ref[...]
    sums = perforation_sums(
        direction, row_ref, col_ref, wrow_ref, wcol_ref, index_ref, wscaled_ref, storage.shape[0]
    )
    put_message(direction, [sums, storage], message_ref, far_ref)
    kind_ref[...] = jnp.full(kind_ref.shape, (gx ^ (gx >> 1) ^ (gi >> 1)) & 1, jnp.int32)


def sweep_kernel(*refs, keep, gain, first, sides):
    (
        residual_ref, direction_ref, pressure_ref, diagonal_ref, inverse_ref,
        til_ref, tiu_ref, txl_ref, txu_ref, zlow_ref, zup_ref,
    ) = refs[:11]
    inline_faces = [ref[...] for ref in refs[11 : 11 + sides[0]]]
    xline_faces = [ref[...] for ref in refs[11 + sides[0] : 11 + sum(sides)]]
    sums_ref, storage_ref, row_ref, col_ref, wrow_ref, wcol_ref, index_ref, *rest = refs[11 + sum(sides) :]
    last = keep is None
    if last:
        next_pressure_ref, next_residual_ref, scaled_ref = rest
    else:
        (
            next_pressure_ref, next_residual_ref, next_direction_ref, message_ref, far_ref,
            scaled_ref, wscaled_ref,
        ) = rest
    wells = sums_ref.shape[0]
    direction = direction_ref[...]
    ilow, iup = neighbours(direction, *halo("inline", inline_faces), 0)
    xlow, xup = neighbours(direction, *halo("xline", xline_faces), 1)
    below, above = layers(direction)
    beside = (
        til_ref[...] * ilow + tiu_ref[...] * iup + txl_ref[...] * xlow + txu_ref[...] * xup
        + zlow_ref[...] * below + zup_ref[...] * above
    )
    if first:
        next_pressure_ref[...] = direction
    else:
        next_pressure_ref[...] = pressure_ref[...] + direction
    next_residual_ref[...] = residual_ref[...] - (diagonal_ref[...] * direction - beside)
    bottom = sums_ref[...] / (1.0 + storage_ref[...])
    spare = wrow_ref.shape[0] - wells
    if spare:
        bottom = jnp.concatenate([bottom, jnp.zeros((spare, LANES), jnp.float32)], axis=0)
    table = stack_split(bottom)
    for part in parts(row_ref.shape[1]):
        values = picked_sum(wrow_ref[:, part], halves_sum(dot_nn(table, wcol_ref[:, part])))
        put_scaled(index_ref[:, part] * values, col_ref, scaled_ref, part)
    wells_term = cells_sum(None, row_ref, col_ref, scaled_ref).reshape(direction_ref.shape)
    residual = next_residual_ref[...] + wells_term
    next_residual_ref[...] = residual
    if not last:
        following = keep * direction_ref[...] + gain * (residual * inverse_ref[...])
        next_direction_ref[...] = following
        next_sums = perforation_sums(
            following, row_ref, col_ref, wrow_ref, wcol_ref, index_ref, wscaled_ref, wells
        )
        put_message(following, [next_sums], message_ref, far_ref)


def body(
    right_side,
    facies,
    facies_table,
    thickness,
    accumulation,
    perforation_cell,
    perf_owner,
    perf_well,
    perf_index,
):
    shape = right_side.shape
    f32 = jnp.float32
    grid = jax.ShapeDtypeStruct(shape, f32)
    n_perf = perforation_cell.shape[0]
    n_dev = lax.axis_size("inline") * lax.axis_size("xline")
    wells = -(-n_dev * WELL_DEV // (8 * LANES)) * 8
    wells_hot = -(-wells // 16) * 16
    sums = jax.ShapeDtypeStruct((wells, LANES), f32)
    faces = [jax.ShapeDtypeStruct((size, LANES), f32) for size in (shape[1], shape[1], shape[0], shape[0])]
    cell = perforation_cell.reshape(1, n_perf)
    owner = perf_owner.reshape(1, n_perf)
    well = perf_well.reshape(1, n_perf)
    index = perf_index.reshape(1, n_perf)
    rows = shape[0] * shape[1]
    hots = tuple(jax.ShapeDtypeStruct((size, n_perf), jnp.bfloat16) for size in (rows, LANES, wells_hot, LANES))
    scaled_scratch = pltpu.VMEM((2 * LANES, n_perf), jnp.bfloat16)
    wscaled_scratch = pltpu.VMEM((2 * wells_hot, n_perf), jnp.bfloat16)

    row_i32 = jax.ShapeDtypeStruct((1, n_perf), jnp.int32)
    row_f32 = jax.ShapeDtypeStruct((1, n_perf), f32)
    ia, ib, xa, xb, lateral, vertical, right_side, accumulation, cell, number, index = pl.pallas_call(
        load_kernel,
        out_shape=(*faces, grid, grid, grid, grid, row_i32, row_i32, row_f32),
        in_specs=[HBM] * 9,
        out_specs=(VMEM,) * 11,
        scratch_shapes=[
            pltpu.SMEM(facies_table.shape, f32),
            pltpu.VMEM(shape, jnp.int32),
            pltpu.VMEM(shape, f32),
            pltpu.VMEM((1, n_perf), jnp.int32),
            pltpu.VMEM((1, n_perf), jnp.int32),
            pltpu.SemaphoreType.DMA((9,)),
        ],
        compiler_params=SMALL,
    )(*(
        pltpu.with_memory_space_constraint(value, pltpu.HBM)
        for value in (facies_table, facies, thickness, right_side, accumulation, cell, owner, well, index)
    ))
    cellwi, storage, zlow, zup, *hot, xa = pl.pallas_call(
        perforation_kernel,
        out_shape=(grid, sums, grid, grid, *hots, faces[2]),
        in_specs=[VMEM] * 5,
        out_specs=(VMEM,) * 9,
        scratch_shapes=[scaled_scratch, wscaled_scratch],
        compiler_params=PARAMS,
    )(vertical, cell, number, index, xa)
    lateral_faces = side_exchange(ia, ib, xa, xb)

    theta = (HIGH_BOUND + LOW_BOUND) / 2.0
    delta = (HIGH_BOUND - LOW_BOUND) / 2.0
    sigma = theta / delta
    rho_now = 1.0 / sigma
    face_rows = shape[0] + 2 * shape[1]
    start_message = jax.ShapeDtypeStruct((2 * wells + face_rows, LANES), f32)
    sweep_message = jax.ShapeDtypeStruct((wells + face_rows, LANES), f32)
    kinds = jax.ShapeDtypeStruct((wells, LANES), jnp.int32)
    til, tiu, txl, txu, diagonal, inverse, direction, message, far, kind = pl.pallas_call(
        functools.partial(start_kernel, scale=1.0 / theta),
        out_shape=(grid,) * 7 + (start_message, faces[2], kinds),
        in_specs=[VMEM] * 16,
        out_specs=(VMEM,) * 10,
        scratch_shapes=[wscaled_scratch],
        compiler_params=PARAMS,
    )(right_side, lateral, accumulation, cellwi, zlow, zup, *lateral_faces, storage, *hot, index)

    residual, pressure = right_side, right_side
    for sweep in range(SWEEPS):
        last = sweep + 1 == SWEEPS
        if sweep == 0:
            both, inline_faces, xline_faces = all_sum(message, far, 2 * wells, kind if two_kinds() else None)
            total, storage = both[:wells], both[wells:]
        else:
            total, inline_faces, xline_faces = all_sum(message, far, wells)
        keep = gain = None
        if not last:
            rho_next = 1.0 / (2.0 * sigma - rho_now)
            keep, gain = rho_next * rho_now, 2.0 * rho_next / delta
            rho_now = rho_next
        sides = (len(inline_faces), len(xline_faces))
        results = pl.pallas_call(
            functools.partial(sweep_kernel, keep=keep, gain=gain, first=sweep == 0, sides=sides),
            out_shape=(grid, grid) if last else (grid, grid, grid, sweep_message, faces[2]),
            in_specs=[VMEM] * (18 + sum(sides)),
            out_specs=(VMEM,) * (2 if last else 5),
            scratch_shapes=[scaled_scratch] if last else [scaled_scratch, wscaled_scratch],
            compiler_params=PARAMS,
        )(residual, direction, pressure, diagonal, inverse, til, tiu, txl, txu, zlow, zup,
          *inline_faces, *xline_faces, total, storage, *hot, index)
        if last:
            pressure, residual = results
        else:
            pressure, residual, direction, message, far = results
    return pressure, residual


def solution(mesh):
    in_specs = (
        P("inline", "xline", None),
        P("inline", "xline", None),
        P(),
        P("inline", "xline", None),
        P("inline", "xline", None),
        P(("inline", "xline")),
        P(("inline", "xline"), None),
        P(("inline", "xline")),
        P(("inline", "xline")),
    )
    out_specs = (P("inline", "xline", None), P("inline", "xline", None))
    return jax.shard_map(body, mesh=mesh, in_specs=in_specs, out_specs=out_specs, check_vma=False)
```

```python
import functools

import jax
import jax.numpy as jnp
from jax import lax
from jax.experimental import pallas as pl
from jax.experimental.pallas import tpu as pltpu
from jax.sharding import PartitionSpec as P

SWEEPS = 3
WELL_DEV = 160
LANES = 128
LOW_BOUND = 0.1
HIGH_BOUND = 2.0
CHUNK = 512
MESH_AXES = ("inline", "xline")

VMEM = pl.BlockSpec(memory_space=pltpu.VMEM)
HBM = pl.BlockSpec(memory_space=pltpu.HBM)
PARAMS = pltpu.CompilerParams(vmem_limit_bytes=16 * 1024 * 1024)
SMALL = pltpu.CompilerParams(vmem_limit_bytes=4 * 1024 * 1024)


def pair_permute(value, partner):
    ni, nx = lax.axis_size("inline"), lax.axis_size("xline")
    pairs = []
    for i in range(ni):
        for j in range(nx):
            i2, j2 = partner(i, j)
            pairs.append((i * nx + j, i2 * nx + j2))
    return lax.ppermute(value, MESH_AXES, pairs)


def xor_permute(value, inline_mask, xline_mask):
    return pair_permute(value, lambda i, j: (i ^ inline_mask, j ^ xline_mask))


def bits_of(count):
    bits = count.bit_length() - 1
    if 1 << bits != count:
        raise ValueError("axis size")
    return bits


def side_masks(count):
    return [(2 << s) - 1 for s in range(bits_of(count))]


def stages_of(count):
    bits = bits_of(count)
    cuts = ([1] if bits % 2 else []) + [2] * (bits // 2)
    stages, low = [], 0
    for width in cuts:
        stages.append([pattern << low | (1 << low) - 1 for pattern in range(1, 1 << width)])
        low += width
    return stages


def all_stages():
    return [[(0, mask) for mask in masks] for masks in stages_of(lax.axis_size("xline"))] + [
        [(mask, 1) for mask in masks] for masks in stages_of(lax.axis_size("inline"))
    ]


SPLIT_STAGES = [[(0, 1)], [(0, 3), (0, 4), (0, 7)], [(1, 0), (2, 1), (3, 1)]]


def two_kinds():
    return [len(stage) for stage in all_stages()] == [len(stage) for stage in SPLIT_STAGES]


def exchange_stage(value, stage, riders, arrived):
    rows = value.shape[0]
    total = value
    for masks in stage:
        rider = riders.get(masks)
        if rider is None:
            got = xor_permute(value, *masks)
        else:
            got = xor_permute(jnp.concatenate([value, rider], axis=0), *masks)
            arrived[masks] = got[rows:]
        total = total + got[:rows]
    return total


def all_sum(message, far, rows, kind=None):
    ni, nx = lax.axis_size("inline"), lax.axis_size("xline")
    lines = far.shape[0]
    first, *others = all_stages()
    if kind is not None:
        others = SPLIT_STAGES[1:]
    got = xor_permute(message, 0, 1)
    value = message[:rows] + got[:rows]
    own = jnp.split(message[rows + lines :], 2, axis=0)
    mate = jnp.split(got[rows + lines :], 2, axis=0)
    arrived = {(0, 1): got[rows : rows + lines]}
    riders = {(0, mask): far for mask in range(2, nx)}
    for stage in others:
        for mask, flip in stage:
            if mask in side_masks(ni):
                riders[mask, flip] = (mate if flip else own)[0 if mask == 1 else 1]
    value = exchange_more(value, message[:rows], first, riders, arrived)
    if kind is not None:
        half = rows // 2
        value = jnp.where(kind == 0, value[:half], value[half:])
    for stage in others:
        value = exchange_stage(value, stage, riders, arrived)
    if kind is not None:
        swapped = xor_permute(value, 0, 1)
        value = jnp.concatenate(
            [jnp.where(kind == 0, value, swapped), jnp.where(kind == 0, swapped, value)], axis=0
        )
    beside = {masks[0] or -masks[1]: face for masks, face in arrived.items()}
    return (
        value,
        [beside[mask] for mask in side_masks(ni)],
        [beside[-mask] for mask in side_masks(nx)],
    )


def exchange_more(value, own, first, riders, arrived):
    rows = own.shape[0]
    for masks in first[1:]:
        rider = riders.get(masks)
        got = xor_permute(own if rider is None else jnp.concatenate([own, rider], axis=0), *masks)
        if rider is not None:
            arrived[masks] = got[rows:]
        value = value + got[:rows]
    return value


def beyond(index, count):
    other = index - 1 if index % 2 == 0 else index + 1
    return other if 0 <= other < count else None


def side_exchange(ia, ib, xa, xb):
    ni, nx = lax.axis_size("inline"), lax.axis_size("xline")

    def inline_far(i, j):
        other = beyond(i, ni)
        return (i, j ^ 1) if other is None else (other, j)

    def xline_far(i, j):
        other = beyond(j, nx)
        return (i ^ 1, j) if other is None else (i, other)

    return (
        xor_permute(ia, 1, 0), pair_permute(ib, inline_far),
        xor_permute(xa, 0, 1), pair_permute(xb, xline_far),
    )


def harmonic_average(first, second):
    return 2.0 * first * second / (first + second)


def split2(value):
    high = value.astype(jnp.bfloat16)
    low = (value - high.astype(jnp.float32)).astype(jnp.bfloat16)
    return high, low


def stack_split(value):
    return jnp.concatenate(split2(value), axis=0)


def dot_nt(a, b):
    return lax.dot_general(a, b, (((1,), (1,)), ((), ())), preferred_element_type=jnp.float32)


def dot_nn(a, b):
    return lax.dot_general(a, b, (((1,), (0,)), ((), ())), preferred_element_type=jnp.float32)


def halves_sum(both):
    half = both.shape[0] // 2
    return both[:half] + both[half:]


def one_hot(index_row, rows):
    shape = (rows, index_row.shape[1])
    hit = lax.broadcasted_iota(jnp.int32, shape, 0) == index_row
    return jnp.where(hit, 1.0, 0.0).astype(jnp.bfloat16)


def scaled(hot, values):
    rows, count = hot.shape
    tiles = hot.reshape(rows // 16, 16, count)
    pieces = split2(jnp.broadcast_to(values, (16, count)))
    return [(tiles * piece[None]).reshape(rows, count) for piece in pieces]


def picked_sum(hot, values):
    return jnp.sum(hot.astype(jnp.float32) * values, axis=0, keepdims=True)


def parts(count):
    return [pl.ds(start, CHUNK) for start in range(0, count, CHUNK)]


def lookup(facies, table_ref, row):
    result = jnp.full(facies.shape, table_ref[row, 0], jnp.float32)
    for entry in range(1, table_ref.shape[1]):
        result = jnp.where(facies == entry, table_ref[row, entry], result)
    return result


def neighbours(cells, lower, upper, dim):
    if dim == 0:
        return (
            jnp.concatenate([lower[None], cells[:-1]], axis=0),
            jnp.concatenate([cells[1:], upper[None]], axis=0),
        )
    size = cells.shape[1]
    place = lax.broadcasted_iota(jnp.int32, cells.shape, 1)
    return (
        jnp.where(place == 0, lower[:, None], pltpu.roll(cells, 1, 1)),
        jnp.where(place == size - 1, upper[:, None], pltpu.roll(cells, size - 1, 1)),
    )


def layers(cells):
    return pltpu.roll(cells, 1, 2), pltpu.roll(cells, LANES - 1, 2)


def side_faces(cells, axis):
    lower, upper = (cells[0], cells[-1]) if axis == "inline" else (cells[:, 0], cells[:, -1])
    odd = lax.axis_index(axis) % 2 == 1
    return jnp.where(odd, lower, upper), jnp.where(odd, upper, lower)


def halo(axis, faces):
    index = lax.axis_index(axis)
    even = index % 2 == 0
    apart = index ^ jnp.where(even, index - 1, index + 1)
    far = faces[-1]
    for mask, face in list(zip(side_masks(lax.axis_size(axis)), faces))[1:-1]:
        far = jnp.where(apart == mask, face, far)
    return jnp.where(even, far, faces[0]), jnp.where(even, faces[0], far)


def put_message(direction, blocks, message_ref, far_ref):
    ia, ib = side_faces(direction, "inline")
    xa, xb = side_faces(direction, "xline")
    start = 0
    for block in (*blocks, xa, ia, ib):
        message_ref[start : start + block.shape[0], :] = block
        start += block.shape[0]
    far_ref[...] = xb


def load_kernel(
    table_hbm, facies_hbm, thickness_hbm, right_hbm, accumulation_hbm, cell_hbm, owner_hbm, well_hbm, index_hbm,
    ia_ref, ib_ref, xa_ref, xb_ref, lateral_ref, vertical_ref,
    right_ref, accumulation_ref, cell_ref, number_ref, index_ref,
    table_ref, facies_ref, thickness_ref, owner_ref, well_ref, sems,
):
    copies = [
        pltpu.make_async_copy(source, target, sems.at[slot])
        for slot, (source, target) in enumerate(
            (
                (table_hbm, table_ref), (facies_hbm, facies_ref), (thickness_hbm, thickness_ref),
                (owner_hbm, owner_ref), (well_hbm, well_ref), (right_hbm, right_ref),
                (accumulation_hbm, accumulation_ref), (cell_hbm, cell_ref), (index_hbm, index_ref),
            )
        )
    ]
    for copy in copies:
        copy.start()
    for copy in copies[:3]:
        copy.wait()
    facies, thickness = facies_ref[...], thickness_ref[...]
    lateral = lookup(facies, table_ref, 0) * thickness
    lateral_ref[...] = lateral
    vertical_ref[...] = lookup(facies, table_ref, 1) / thickness
    ia_ref[...], ib_ref[...] = side_faces(lateral, "inline")
    xa_ref[...], xb_ref[...] = side_faces(lateral, "xline")
    for copy in copies[3:]:
        copy.wait()
    number_ref[...] = owner_ref[...] * WELL_DEV + well_ref[...]


def perforation_kernel(
    vertical_ref, cell_ref, number_ref, index_ref, face_ref,
    cellwi_ref, storage_ref, zlow_ref, zup_ref, row_ref, col_ref, wrow_ref, wcol_ref, face_out_ref,
    scaled_ref, wscaled_ref,
):
    face_out_ref[...] = face_ref[...]
    vertical = vertical_ref[...]
    below, above = layers(vertical)
    place = lax.broadcasted_iota(jnp.int32, vertical.shape, 2)
    zlow_ref[...] = jnp.where(place == 0, 0.0, harmonic_average(vertical, below))
    zup_ref[...] = jnp.where(place == LANES - 1, 0.0, harmonic_average(vertical, above))
    for part in parts(cell_ref.shape[1]):
        cell, number = cell_ref[:, part], number_ref[:, part]
        row_ref[:, part] = one_hot(cell >> 7, row_ref.shape[0])
        col_ref[:, part] = one_hot(cell & (LANES - 1), LANES)
        wrow_ref[:, part] = one_hot(number >> 7, wrow_ref.shape[0])
        wcol_ref[:, part] = one_hot(number & (LANES - 1), LANES)
    cellwi_ref[...] = cells_sum(index_ref, row_ref, col_ref, scaled_ref).reshape(cellwi_ref.shape)
    for part in parts(cell_ref.shape[1]):
        put_wells(index_ref[:, part], wrow_ref, wscaled_ref, part)
    storage_ref[...] = wells_sum(wscaled_ref, wcol_ref, storage_ref.shape[0])


def put_scaled(values, col_ref, scaled_ref, part):
    scaled_ref[0:LANES, part], scaled_ref[LANES:, part] = scaled(col_ref[:, part], values)


def cells_sum(values_ref, row_ref, col_ref, scaled_ref):
    if values_ref is not None:
        for part in parts(row_ref.shape[1]):
            put_scaled(values_ref[:, part], col_ref, scaled_ref, part)
    both = dot_nt(row_ref[...], scaled_ref[...])
    return both[:, :LANES] + both[:, LANES:]


def put_wells(values, wrow_ref, wscaled_ref, part):
    rows = wrow_ref.shape[0]
    wscaled_ref[0:rows, part], wscaled_ref[rows:, part] = scaled(wrow_ref[:, part], values)


def wells_sum(wscaled_ref, wcol_ref, wells):
    return halves_sum(dot_nt(wscaled_ref[...], wcol_ref[...]))[:wells]


def perforation_sums(direction, row_ref, col_ref, wrow_ref, wcol_ref, index_ref, wscaled_ref, wells):
    fieldt = stack_split(direction.reshape(-1, LANES).T)
    for part in parts(row_ref.shape[1]):
        values = picked_sum(col_ref[:, part], halves_sum(dot_nn(fieldt, row_ref[:, part])))
        put_wells(index_ref[:, part] * values, wrow_ref, wscaled_ref, part)
    return wells_sum(wscaled_ref, wcol_ref, wells)


def start_kernel(
    right_ref, lateral_ref, accumulation_ref, cellwi_ref, zlow_ref, zup_ref,
    ia_ref, ib_ref, xa_ref, xb_ref, storage_ref, row_ref, col_ref, wrow_ref, wcol_ref, index_ref,
    til_ref, tiu_ref, txl_ref, txu_ref, diagonal_ref, inverse_ref, direction_ref, message_ref, far_ref, kind_ref,
    wscaled_ref,
    *, scale,
):
    lateral = lateral_ref[...]
    gi, gx = lax.axis_index("inline"), lax.axis_index("xline")
    low, up = halo("inline", [ia_ref[...], ib_ref[...]])
    low = jnp.where(gi == 0, 0.0, low)
    up = jnp.where(gi == lax.axis_size("inline") - 1, 0.0, up)
    low, up = neighbours(lateral, low, up, 0)
    til, tiu = harmonic_average(lateral, low), harmonic_average(lateral, up)
    low, up = halo("xline", [xa_ref[...], xb_ref[...]])
    low = jnp.where(gx == 0, 0.0, low)
    up = jnp.where(gx == lax.axis_size("xline") - 1, 0.0, up)
    low, up = neighbours(lateral, low, up, 1)
    txl, txu = harmonic_average(lateral, low), harmonic_average(lateral, up)
    til_ref[...], tiu_ref[...], txl_ref[...], txu_ref[...] = til, tiu, txl, txu
    diagonal = accumulation_ref[...] + til + tiu + txl + txu + zlow_ref[...] + zup_ref[...] + cellwi_ref[...]
    inverse = 1.0 / diagonal
    direction = right_ref[...] * inverse * scale
    diagonal_ref[...] = diagonal
    inverse_ref[...] = inverse
    direction_ref[...] = direction
    storage = storage_ref[...]
    sums = perforation_sums(
        direction, row_ref, col_ref, wrow_ref, wcol_ref, index_ref, wscaled_ref, storage.shape[0]
    )
    put_message(direction, [sums, storage], message_ref, far_ref)
    kind_ref[...] = jnp.full(kind_ref.shape, (gx ^ (gx >> 1) ^ (gi >> 1)) & 1, jnp.int32)


def sweep_kernel(*refs, keep, gain, first, sides):
    (
        residual_ref, direction_ref, pressure_ref, diagonal_ref, inverse_ref,
        til_ref, tiu_ref, txl_ref, txu_ref, zlow_ref, zup_ref,
    ) = refs[:11]
    inline_faces = [ref[...] for ref in refs[11 : 11 + sides[0]]]
    xline_faces = [ref[...] for ref in refs[11 + sides[0] : 11 + sum(sides)]]
    sums_ref, storage_ref, row_ref, col_ref, wrow_ref, wcol_ref, index_ref, *rest = refs[11 + sum(sides) :]
    last = keep is None
    if last:
        next_pressure_ref, next_residual_ref, scaled_ref = rest
    else:
        (
            next_pressure_ref, next_residual_ref, next_direction_ref, message_ref, far_ref,
            scaled_ref, wscaled_ref,
        ) = rest
    wells = sums_ref.shape[0]
    direction = direction_ref[...]
    ilow, iup = neighbours(direction, *halo("inline", inline_faces), 0)
    xlow, xup = neighbours(direction, *halo("xline", xline_faces), 1)
    below, above = layers(direction)
    beside = (
        til_ref[...] * ilow + tiu_ref[...] * iup + txl_ref[...] * xlow + txu_ref[...] * xup
        + zlow_ref[...] * below + zup_ref[...] * above
    )
    if first:
        next_pressure_ref[...] = direction
    else:
        next_pressure_ref[...] = pressure_ref[...] + direction
    next_residual_ref[...] = residual_ref[...] - (diagonal_ref[...] * direction - beside)
    bottom = sums_ref[...] / (1.0 + storage_ref[...])
    spare = wrow_ref.shape[0] - wells
    if spare:
        bottom = jnp.concatenate([bottom, jnp.zeros((spare, LANES), jnp.float32)], axis=0)
    table = stack_split(bottom)
    for part in parts(row_ref.shape[1]):
        values = picked_sum(wrow_ref[:, part], halves_sum(dot_nn(table, wcol_ref[:, part])))
        put_scaled(index_ref[:, part] * values, col_ref, scaled_ref, part)
    wells_term = cells_sum(None, row_ref, col_ref, scaled_ref).reshape(direction_ref.shape)
    residual = next_residual_ref[...] + wells_term
    next_residual_ref[...] = residual
    if not last:
        following = keep * direction_ref[...] + gain * (residual * inverse_ref[...])
        next_direction_ref[...] = following
        next_sums = perforation_sums(
            following, row_ref, col_ref, wrow_ref, wcol_ref, index_ref, wscaled_ref, wells
        )
        put_message(following, [next_sums], message_ref, far_ref)


def body(
    right_side,
    facies,
    facies_table,
    thickness,
    accumulation,
    perforation_cell,
    perf_owner,
    perf_well,
    perf_index,
):
    shape = right_side.shape
    f32 = jnp.float32
    grid = jax.ShapeDtypeStruct(shape, f32)
    n_perf = perforation_cell.shape[0]
    n_dev = lax.axis_size("inline") * lax.axis_size("xline")
    wells = -(-n_dev * WELL_DEV // (8 * LANES)) * 8
    wells_hot = -(-wells // 16) * 16
    sums = jax.ShapeDtypeStruct((wells, LANES), f32)
    faces = [jax.ShapeDtypeStruct((size, LANES), f32) for size in (shape[1], shape[1], shape[0], shape[0])]
    cell = perforation_cell.reshape(1, n_perf)
    owner = perf_owner.reshape(1, n_perf)
    well = perf_well.reshape(1, n_perf)
    index = perf_index.reshape(1, n_perf)
    rows = shape[0] * shape[1]
    hots = tuple(jax.ShapeDtypeStruct((size, n_perf), jnp.bfloat16) for size in (rows, LANES, wells_hot, LANES))
    scaled_scratch = pltpu.VMEM((2 * LANES, n_perf), jnp.bfloat16)
    wscaled_scratch = pltpu.VMEM((2 * wells_hot, n_perf), jnp.bfloat16)

    row_i32 = jax.ShapeDtypeStruct((1, n_perf), jnp.int32)
    row_f32 = jax.ShapeDtypeStruct((1, n_perf), f32)
    ia, ib, xa, xb, lateral, vertical, right_side, accumulation, cell, number, index = pl.pallas_call(
        load_kernel,
        out_shape=(*faces, grid, grid, grid, grid, row_i32, row_i32, row_f32),
        in_specs=[HBM] * 9,
        out_specs=(VMEM,) * 11,
        scratch_shapes=[
            pltpu.SMEM(facies_table.shape, f32),
            pltpu.VMEM(shape, jnp.int32),
            pltpu.VMEM(shape, f32),
            pltpu.VMEM((1, n_perf), jnp.int32),
            pltpu.VMEM((1, n_perf), jnp.int32),
            pltpu.SemaphoreType.DMA((9,)),
        ],
        compiler_params=SMALL,
    )(*(
        pltpu.with_memory_space_constraint(value, pltpu.HBM)
        for value in (facies_table, facies, thickness, right_side, accumulation, cell, owner, well, index)
    ))
    cellwi, storage, zlow, zup, *hot, xa = pl.pallas_call(
        perforation_kernel,
        out_shape=(grid, sums, grid, grid, *hots, faces[2]),
        in_specs=[VMEM] * 5,
        out_specs=(VMEM,) * 9,
        scratch_shapes=[scaled_scratch, wscaled_scratch],
        compiler_params=PARAMS,
    )(vertical, cell, number, index, xa)
    lateral_faces = side_exchange(ia, ib, xa, xb)

    theta = (HIGH_BOUND + LOW_BOUND) / 2.0
    delta = (HIGH_BOUND - LOW_BOUND) / 2.0
    sigma = theta / delta
    rho_now = 1.0 / sigma
    face_rows = shape[0] + 2 * shape[1]
    start_message = jax.ShapeDtypeStruct((2 * wells + face_rows, LANES), f32)
    sweep_message = jax.ShapeDtypeStruct((wells + face_rows, LANES), f32)
    kinds = jax.ShapeDtypeStruct((wells, LANES), jnp.int32)
    til, tiu, txl, txu, diagonal, inverse, direction, message, far, kind = pl.pallas_call(
        functools.partial(start_kernel, scale=1.0 / theta),
        out_shape=(grid,) * 7 + (start_message, faces[2], kinds),
        in_specs=[VMEM] * 16,
        out_specs=(VMEM,) * 10,
        scratch_shapes=[wscaled_scratch],
        compiler_params=PARAMS,
    )(right_side, lateral, accumulation, cellwi, zlow, zup, *lateral_faces, storage, *hot, index)

    residual, pressure = right_side, right_side
    for sweep in range(SWEEPS):
        last = sweep + 1 == SWEEPS
        if sweep == 0:
            both, inline_faces, xline_faces = all_sum(message, far, 2 * wells, kind if two_kinds() else None)
            total, storage = both[:wells], both[wells:]
        else:
            total, inline_faces, xline_faces = all_sum(message, far, wells)
        keep = gain = None
        if not last:
            rho_next = 1.0 / (2.0 * sigma - rho_now)
            keep, gain = rho_next * rho_now, 2.0 * rho_next / delta
            rho_now = rho_next
        sides = (len(inline_faces), len(xline_faces))
        results = pl.pallas_call(
            functools.partial(sweep_kernel, keep=keep, gain=gain, first=sweep == 0, sides=sides),
            out_shape=(grid, grid) if last else (grid, grid, grid, sweep_message, faces[2]),
            in_specs=[VMEM] * (18 + sum(sides)),
            out_specs=(VMEM,) * (2 if last else 5),
            scratch_shapes=[scaled_scratch] if last else [scaled_scratch, wscaled_scratch],
            compiler_params=PARAMS,
        )(residual, direction, pressure, diagonal, inverse, til, tiu, txl, txu, zlow, zup,
          *inline_faces, *xline_faces, total, storage, *hot, index)
        if last:
            pressure, residual = results
        else:
            pressure, residual, direction, message, far = results
    return pressure, residual


def solution(mesh):
    in_specs = (
        P("inline", "xline", None),
        P("inline", "xline", None),
        P(),
        P("inline", "xline", None),
        P("inline", "xline", None),
        P(("inline", "xline")),
        P(("inline", "xline"), None),
        P(("inline", "xline")),
        P(("inline", "xline")),
    )
    out_specs = (P("inline", "xline", None), P("inline", "xline", None))
    return jax.shard_map(body, mesh=mesh, in_specs=in_specs, out_specs=out_specs, check_vma=False)
```

```python
import functools

import jax
import jax.numpy as jnp
from jax import lax
from jax.experimental import pallas as pl
from jax.experimental.pallas import tpu as pltpu
from jax.sharding import PartitionSpec as P

SWEEPS = 3
WELL_DEV = 160
LANES = 128
LOW_BOUND = 0.1
HIGH_BOUND = 2.0
CHUNK = 512
MESH_AXES = ("inline", "xline")

VMEM = pl.BlockSpec(memory_space=pltpu.VMEM)
HBM = pl.BlockSpec(memory_space=pltpu.HBM)
PARAMS = pltpu.CompilerParams(vmem_limit_bytes=16 * 1024 * 1024)
SMALL = pltpu.CompilerParams(vmem_limit_bytes=4 * 1024 * 1024)


def pair_permute(value, partner):
    ni, nx = lax.axis_size("inline"), lax.axis_size("xline")
    pairs = []
    for i in range(ni):
        for j in range(nx):
            i2, j2 = partner(i, j)
            pairs.append((i * nx + j, i2 * nx + j2))
    return lax.ppermute(value, MESH_AXES, pairs)


def xor_permute(value, inline_mask, xline_mask):
    return pair_permute(value, lambda i, j: (i ^ inline_mask, j ^ xline_mask))


def bits_of(count):
    bits = count.bit_length() - 1
    if 1 << bits != count:
        raise ValueError("axis size")
    return bits


def side_masks(count):
    return [(2 << s) - 1 for s in range(bits_of(count))]


def stages_of(count):
    bits = bits_of(count)
    cuts = ([1] if bits % 2 else []) + [2] * (bits // 2)
    stages, low = [], 0
    for width in cuts:
        stages.append([pattern << low | (1 << low) - 1 for pattern in range(1, 1 << width)])
        low += width
    return stages


def all_stages():
    return [[(0, mask) for mask in masks] for masks in stages_of(lax.axis_size("xline"))] + [
        [(mask, 1) for mask in reversed(masks)] for masks in stages_of(lax.axis_size("inline"))
    ]


SPLIT_STAGES = [[(0, 1)], [(0, 3), (0, 4), (0, 7)], [(3, 1), (2, 1), (1, 0)]]


def two_kinds():
    return [len(stage) for stage in all_stages()] == [len(stage) for stage in SPLIT_STAGES]


def exchange_stage(value, stage, riders, arrived):
    rows = value.shape[0]
    total = value
    for masks in stage:
        rider = riders.get(masks)
        if rider is None:
            got = xor_permute(value, *masks)
        else:
            got = xor_permute(jnp.concatenate([value, rider], axis=0), *masks)
            arrived[masks] = got[rows:]
        total = total + got[:rows]
    return total


def all_sum(message, far, rows, kind=None):
    ni, nx = lax.axis_size("inline"), lax.axis_size("xline")
    lines = far.shape[0]
    first, *others = all_stages()
    if kind is not None:
        others = SPLIT_STAGES[1:]
    got = xor_permute(message, 0, 1)
    value = message[:rows] + got[:rows]
    own = jnp.split(message[rows + lines :], 2, axis=0)
    mate = jnp.split(got[rows + lines :], 2, axis=0)
    arrived = {(0, 1): got[rows : rows + lines]}
    riders = {(0, mask): far for mask in range(2, nx)}
    for stage in others:
        for mask, flip in stage:
            if mask in side_masks(ni):
                riders[mask, flip] = (mate if flip else own)[0 if mask == 1 else 1]
    value = exchange_more(value, message[:rows], first, riders, arrived)
    if kind is not None:
        half = rows // 2
        value = jnp.where(kind == 0, value[:half], value[half:])
    for stage in others:
        value = exchange_stage(value, stage, riders, arrived)
    if kind is not None:
        swapped = xor_permute(value, 0, 1)
        value = jnp.concatenate(
            [jnp.where(kind == 0, value, swapped), jnp.where(kind == 0, swapped, value)], axis=0
        )
    beside = {masks[0] or -masks[1]: face for masks, face in arrived.items()}
    return (
        value,
        [beside[mask] for mask in side_masks(ni)],
        [beside[-mask] for mask in side_masks(nx)],
    )


def exchange_more(value, own, first, riders, arrived):
    rows = own.shape[0]
    for masks in first[1:]:
        rider = riders.get(masks)
        got = xor_permute(own if rider is None else jnp.concatenate([own, rider], axis=0), *masks)
        if rider is not None:
            arrived[masks] = got[rows:]
        value = value + got[:rows]
    return value


def beyond(index, count):
    other = index - 1 if index % 2 == 0 else index + 1
    return other if 0 <= other < count else None


def side_exchange(ia, ib, xa, xb):
    ni, nx = lax.axis_size("inline"), lax.axis_size("xline")

    def inline_far(i, j):
        other = beyond(i, ni)
        return (i, j ^ 1) if other is None else (other, j)

    def xline_far(i, j):
        other = beyond(j, nx)
        return (i ^ 1, j) if other is None else (i, other)

    return (
        xor_permute(ia, 1, 0), pair_permute(ib, inline_far),
        xor_permute(xa, 0, 1), pair_permute(xb, xline_far),
    )


def harmonic_average(first, second):
    return 2.0 * first * second / (first + second)


def split2(value):
    high = value.astype(jnp.bfloat16)
    low = (value - high.astype(jnp.float32)).astype(jnp.bfloat16)
    return high, low


def stack_split(value):
    return jnp.concatenate(split2(value), axis=0)


def dot_nt(a, b):
    return lax.dot_general(a, b, (((1,), (1,)), ((), ())), preferred_element_type=jnp.float32)


def dot_nn(a, b):
    return lax.dot_general(a, b, (((1,), (0,)), ((), ())), preferred_element_type=jnp.float32)


def halves_sum(both):
    half = both.shape[0] // 2
    return both[:half] + both[half:]


def one_hot(index_row, rows):
    shape = (rows, index_row.shape[1])
    hit = lax.broadcasted_iota(jnp.int32, shape, 0) == index_row
    return jnp.where(hit, 1.0, 0.0).astype(jnp.bfloat16)


def scaled(hot, values):
    rows, count = hot.shape
    tiles = hot.reshape(rows // 16, 16, count)
    pieces = split2(jnp.broadcast_to(values, (16, count)))
    return [(tiles * piece[None]).reshape(rows, count) for piece in pieces]


def picked_sum(hot, values):
    return jnp.sum(hot.astype(jnp.float32) * values, axis=0, keepdims=True)


def parts(count):
    return [pl.ds(start, CHUNK) for start in range(0, count, CHUNK)]


def lookup(facies, table_ref, row):
    result = jnp.full(facies.shape, table_ref[row, 0], jnp.float32)
    for entry in range(1, table_ref.shape[1]):
        result = jnp.where(facies == entry, table_ref[row, entry], result)
    return result


def neighbours(cells, lower, upper, dim):
    if dim == 0:
        return (
            jnp.concatenate([lower[None], cells[:-1]], axis=0),
            jnp.concatenate([cells[1:], upper[None]], axis=0),
        )
    size = cells.shape[1]
    place = lax.broadcasted_iota(jnp.int32, cells.shape, 1)
    return (
        jnp.where(place == 0, lower[:, None], pltpu.roll(cells, 1, 1)),
        jnp.where(place == size - 1, upper[:, None], pltpu.roll(cells, size - 1, 1)),
    )


def layers(cells):
    return pltpu.roll(cells, 1, 2), pltpu.roll(cells, LANES - 1, 2)


def side_faces(cells, axis):
    lower, upper = (cells[0], cells[-1]) if axis == "inline" else (cells[:, 0], cells[:, -1])
    odd = lax.axis_index(axis) % 2 == 1
    return jnp.where(odd, lower, upper), jnp.where(odd, upper, lower)


def halo(axis, faces):
    index = lax.axis_index(axis)
    even = index % 2 == 0
    apart = index ^ jnp.where(even, index - 1, index + 1)
    far = faces[-1]
    for mask, face in list(zip(side_masks(lax.axis_size(axis)), faces))[1:-1]:
        far = jnp.where(apart == mask, face, far)
    return jnp.where(even, far, faces[0]), jnp.where(even, faces[0], far)


def put_message(direction, blocks, message_ref, far_ref):
    ia, ib = side_faces(direction, "inline")
    xa, xb = side_faces(direction, "xline")
    start = 0
    for block in (*blocks, xa, ia, ib):
        message_ref[start : start + block.shape[0], :] = block
        start += block.shape[0]
    far_ref[...] = xb


def load_kernel(
    table_hbm, facies_hbm, thickness_hbm, right_hbm, accumulation_hbm, cell_hbm, owner_hbm, well_hbm, index_hbm,
    ia_ref, ib_ref, xa_ref, xb_ref, lateral_ref, vertical_ref,
    right_ref, accumulation_ref, cell_ref, number_ref, index_ref,
    table_ref, facies_ref, thickness_ref, owner_ref, well_ref, sems,
):
    copies = [
        pltpu.make_async_copy(source, target, sems.at[slot])
        for slot, (source, target) in enumerate(
            (
                (table_hbm, table_ref), (facies_hbm, facies_ref), (thickness_hbm, thickness_ref),
                (owner_hbm, owner_ref), (well_hbm, well_ref), (right_hbm, right_ref),
                (accumulation_hbm, accumulation_ref), (cell_hbm, cell_ref), (index_hbm, index_ref),
            )
        )
    ]
    for copy in copies:
        copy.start()
    for copy in copies[:3]:
        copy.wait()
    facies, thickness = facies_ref[...], thickness_ref[...]
    lateral = lookup(facies, table_ref, 0) * thickness
    lateral_ref[...] = lateral
    vertical_ref[...] = lookup(facies, table_ref, 1) / thickness
    ia_ref[...], ib_ref[...] = side_faces(lateral, "inline")
    xa_ref[...], xb_ref[...] = side_faces(lateral, "xline")
    for copy in copies[3:]:
        copy.wait()
    number_ref[...] = owner_ref[...] * WELL_DEV + well_ref[...]


def perforation_kernel(
    vertical_ref, cell_ref, number_ref, index_ref, face_ref,
    cellwi_ref, storage_ref, zlow_ref, zup_ref, row_ref, col_ref, wrow_ref, wcol_ref, face_out_ref,
    scaled_ref, wscaled_ref,
):
    face_out_ref[...] = face_ref[...]
    vertical = vertical_ref[...]
    below, above = layers(vertical)
    place = lax.broadcasted_iota(jnp.int32, vertical.shape, 2)
    zlow_ref[...] = jnp.where(place == 0, 0.0, harmonic_average(vertical, below))
    zup_ref[...] = jnp.where(place == LANES - 1, 0.0, harmonic_average(vertical, above))
    for part in parts(cell_ref.shape[1]):
        cell, number = cell_ref[:, part], number_ref[:, part]
        row_ref[:, part] = one_hot(cell >> 7, row_ref.shape[0])
        col_ref[:, part] = one_hot(cell & (LANES - 1), LANES)
        wrow_ref[:, part] = one_hot(number >> 7, wrow_ref.shape[0])
        wcol_ref[:, part] = one_hot(number & (LANES - 1), LANES)
    cellwi_ref[...] = cells_sum(index_ref, row_ref, col_ref, scaled_ref).reshape(cellwi_ref.shape)
    for part in parts(cell_ref.shape[1]):
        put_wells(index_ref[:, part], wrow_ref, wscaled_ref, part)
    storage_ref[...] = wells_sum(wscaled_ref, wcol_ref, storage_ref.shape[0])


def put_scaled(values, col_ref, scaled_ref, part):
    scaled_ref[0:LANES, part], scaled_ref[LANES:, part] = scaled(col_ref[:, part], values)


def cells_sum(values_ref, row_ref, col_ref, scaled_ref):
    if values_ref is not None:
        for part in parts(row_ref.shape[1]):
            put_scaled(values_ref[:, part], col_ref, scaled_ref, part)
    both = dot_nt(row_ref[...], scaled_ref[...])
    return both[:, :LANES] + both[:, LANES:]


def put_wells(values, wrow_ref, wscaled_ref, part):
    rows = wrow_ref.shape[0]
    wscaled_ref[0:rows, part], wscaled_ref[rows:, part] = scaled(wrow_ref[:, part], values)


def wells_sum(wscaled_ref, wcol_ref, wells):
    return halves_sum(dot_nt(wscaled_ref[...], wcol_ref[...]))[:wells]


def perforation_sums(direction, row_ref, col_ref, wrow_ref, wcol_ref, index_ref, wscaled_ref, wells):
    fieldt = stack_split(direction.reshape(-1, LANES).T)
    for part in parts(row_ref.shape[1]):
        values = picked_sum(col_ref[:, part], halves_sum(dot_nn(fieldt, row_ref[:, part])))
        put_wells(index_ref[:, part] * values, wrow_ref, wscaled_ref, part)
    return wells_sum(wscaled_ref, wcol_ref, wells)


def start_kernel(
    right_ref, lateral_ref, accumulation_ref, cellwi_ref, zlow_ref, zup_ref,
    ia_ref, ib_ref, xa_ref, xb_ref, storage_ref, row_ref, col_ref, wrow_ref, wcol_ref, index_ref,
    til_ref, tiu_ref, txl_ref, txu_ref, diagonal_ref, inverse_ref, direction_ref, message_ref, far_ref, kind_ref,
    wscaled_ref,
    *, scale,
):
    lateral = lateral_ref[...]
    gi, gx = lax.axis_index("inline"), lax.axis_index("xline")
    low, up = halo("inline", [ia_ref[...], ib_ref[...]])
    low = jnp.where(gi == 0, 0.0, low)
    up = jnp.where(gi == lax.axis_size("inline") - 1, 0.0, up)
    low, up = neighbours(lateral, low, up, 0)
    til, tiu = harmonic_average(lateral, low), harmonic_average(lateral, up)
    low, up = halo("xline", [xa_ref[...], xb_ref[...]])
    low = jnp.where(gx == 0, 0.0, low)
    up = jnp.where(gx == lax.axis_size("xline") - 1, 0.0, up)
    low, up = neighbours(lateral, low, up, 1)
    txl, txu = harmonic_average(lateral, low), harmonic_average(lateral, up)
    til_ref[...], tiu_ref[...], txl_ref[...], txu_ref[...] = til, tiu, txl, txu
    diagonal = accumulation_ref[...] + til + tiu + txl + txu + zlow_ref[...] + zup_ref[...] + cellwi_ref[...]
    inverse = 1.0 / diagonal
    direction = right_ref[...] * inverse * scale
    diagonal_ref[...] = diagonal
    inverse_ref[...] = inverse
    direction_ref[...] = direction
    storage = storage_ref[...]
    sums = perforation_sums(
        direction, row_ref, col_ref, wrow_ref, wcol_ref, index_ref, wscaled_ref, storage.shape[0]
    )
    put_message(direction, [sums, storage], message_ref, far_ref)
    kind_ref[...] = jnp.full(kind_ref.shape, (gx ^ (gx >> 1) ^ (gi >> 1)) & 1, jnp.int32)


def sweep_kernel(*refs, keep, gain, first, sides):
    (
        residual_ref, direction_ref, pressure_ref, diagonal_ref, inverse_ref,
        til_ref, tiu_ref, txl_ref, txu_ref, zlow_ref, zup_ref,
    ) = refs[:11]
    inline_faces = [ref[...] for ref in refs[11 : 11 + sides[0]]]
    xline_faces = [ref[...] for ref in refs[11 + sides[0] : 11 + sum(sides)]]
    sums_ref, storage_ref, row_ref, col_ref, wrow_ref, wcol_ref, index_ref, *rest = refs[11 + sum(sides) :]
    last = keep is None
    if last:
        next_pressure_ref, next_residual_ref, scaled_ref = rest
    else:
        (
            next_pressure_ref, next_residual_ref, next_direction_ref, message_ref, far_ref,
            scaled_ref, wscaled_ref,
        ) = rest
    wells = sums_ref.shape[0]
    direction = direction_ref[...]
    ilow, iup = neighbours(direction, *halo("inline", inline_faces), 0)
    xlow, xup = neighbours(direction, *halo("xline", xline_faces), 1)
    below, above = layers(direction)
    beside = (
        til_ref[...] * ilow + tiu_ref[...] * iup + txl_ref[...] * xlow + txu_ref[...] * xup
        + zlow_ref[...] * below + zup_ref[...] * above
    )
    if first:
        next_pressure_ref[...] = direction
    else:
        next_pressure_ref[...] = pressure_ref[...] + direction
    next_residual_ref[...] = residual_ref[...] - (diagonal_ref[...] * direction - beside)
    bottom = sums_ref[...] / (1.0 + storage_ref[...])
    spare = wrow_ref.shape[0] - wells
    if spare:
        bottom = jnp.concatenate([bottom, jnp.zeros((spare, LANES), jnp.float32)], axis=0)
    table = stack_split(bottom)
    for part in parts(row_ref.shape[1]):
        values = picked_sum(wrow_ref[:, part], halves_sum(dot_nn(table, wcol_ref[:, part])))
        put_scaled(index_ref[:, part] * values, col_ref, scaled_ref, part)
    wells_term = cells_sum(None, row_ref, col_ref, scaled_ref).reshape(direction_ref.shape)
    residual = next_residual_ref[...] + wells_term
    next_residual_ref[...] = residual
    if not last:
        following = keep * direction_ref[...] + gain * (residual * inverse_ref[...])
        next_direction_ref[...] = following
        next_sums = perforation_sums(
            following, row_ref, col_ref, wrow_ref, wcol_ref, index_ref, wscaled_ref, wells
        )
        put_message(following, [next_sums], message_ref, far_ref)


def body(
    right_side,
    facies,
    facies_table,
    thickness,
    accumulation,
    perforation_cell,
    perf_owner,
    perf_well,
    perf_index,
):
    shape = right_side.shape
    f32 = jnp.float32
    grid = jax.ShapeDtypeStruct(shape, f32)
    n_perf = perforation_cell.shape[0]
    n_dev = lax.axis_size("inline") * lax.axis_size("xline")
    wells = -(-n_dev * WELL_DEV // (8 * LANES)) * 8
    wells_hot = -(-wells // 16) * 16
    sums = jax.ShapeDtypeStruct((wells, LANES), f32)
    faces = [jax.ShapeDtypeStruct((size, LANES), f32) for size in (shape[1], shape[1], shape[0], shape[0])]
    cell = perforation_cell.reshape(1, n_perf)
    owner = perf_owner.reshape(1, n_perf)
    well = perf_well.reshape(1, n_perf)
    index = perf_index.reshape(1, n_perf)
    rows = shape[0] * shape[1]
    hots = tuple(jax.ShapeDtypeStruct((size, n_perf), jnp.bfloat16) for size in (rows, LANES, wells_hot, LANES))
    scaled_scratch = pltpu.VMEM((2 * LANES, n_perf), jnp.bfloat16)
    wscaled_scratch = pltpu.VMEM((2 * wells_hot, n_perf), jnp.bfloat16)

    row_i32 = jax.ShapeDtypeStruct((1, n_perf), jnp.int32)
    row_f32 = jax.ShapeDtypeStruct((1, n_perf), f32)
    ia, ib, xa, xb, lateral, vertical, right_side, accumulation, cell, number, index = pl.pallas_call(
        load_kernel,
        out_shape=(*faces, grid, grid, grid, grid, row_i32, row_i32, row_f32),
        in_specs=[HBM] * 9,
        out_specs=(VMEM,) * 11,
        scratch_shapes=[
            pltpu.SMEM(facies_table.shape, f32),
            pltpu.VMEM(shape, jnp.int32),
            pltpu.VMEM(shape, f32),
            pltpu.VMEM((1, n_perf), jnp.int32),
            pltpu.VMEM((1, n_perf), jnp.int32),
            pltpu.SemaphoreType.DMA((9,)),
        ],
        compiler_params=SMALL,
    )(*(
        pltpu.with_memory_space_constraint(value, pltpu.HBM)
        for value in (facies_table, facies, thickness, right_side, accumulation, cell, owner, well, index)
    ))
    cellwi, storage, zlow, zup, *hot, xa = pl.pallas_call(
        perforation_kernel,
        out_shape=(grid, sums, grid, grid, *hots, faces[2]),
        in_specs=[VMEM] * 5,
        out_specs=(VMEM,) * 9,
        scratch_shapes=[scaled_scratch, wscaled_scratch],
        compiler_params=PARAMS,
    )(vertical, cell, number, index, xa)
    lateral_faces = side_exchange(ia, ib, xa, xb)

    theta = (HIGH_BOUND + LOW_BOUND) / 2.0
    delta = (HIGH_BOUND - LOW_BOUND) / 2.0
    sigma = theta / delta
    rho_now = 1.0 / sigma
    face_rows = shape[0] + 2 * shape[1]
    start_message = jax.ShapeDtypeStruct((2 * wells + face_rows, LANES), f32)
    sweep_message = jax.ShapeDtypeStruct((wells + face_rows, LANES), f32)
    kinds = jax.ShapeDtypeStruct((wells, LANES), jnp.int32)
    til, tiu, txl, txu, diagonal, inverse, direction, message, far, kind = pl.pallas_call(
        functools.partial(start_kernel, scale=1.0 / theta),
        out_shape=(grid,) * 7 + (start_message, faces[2], kinds),
        in_specs=[VMEM] * 16,
        out_specs=(VMEM,) * 10,
        scratch_shapes=[wscaled_scratch],
        compiler_params=PARAMS,
    )(right_side, lateral, accumulation, cellwi, zlow, zup, *lateral_faces, storage, *hot, index)

    residual, pressure = right_side, right_side
    for sweep in range(SWEEPS):
        last = sweep + 1 == SWEEPS
        if sweep == 0:
            both, inline_faces, xline_faces = all_sum(message, far, 2 * wells, kind if two_kinds() else None)
            total, storage = both[:wells], both[wells:]
        else:
            total, inline_faces, xline_faces = all_sum(message, far, wells)
        keep = gain = None
        if not last:
            rho_next = 1.0 / (2.0 * sigma - rho_now)
            keep, gain = rho_next * rho_now, 2.0 * rho_next / delta
            rho_now = rho_next
        sides = (len(inline_faces), len(xline_faces))
        results = pl.pallas_call(
            functools.partial(sweep_kernel, keep=keep, gain=gain, first=sweep == 0, sides=sides),
            out_shape=(grid, grid) if last else (grid, grid, grid, sweep_message, faces[2]),
            in_specs=[VMEM] * (18 + sum(sides)),
            out_specs=(VMEM,) * (2 if last else 5),
            scratch_shapes=[scaled_scratch] if last else [scaled_scratch, wscaled_scratch],
            compiler_params=PARAMS,
        )(residual, direction, pressure, diagonal, inverse, til, tiu, txl, txu, zlow, zup,
          *inline_faces, *xline_faces, total, storage, *hot, index)
        if last:
            pressure, residual = results
        else:
            pressure, residual, direction, message, far = results
    return pressure, residual


def solution(mesh):
    in_specs = (
        P("inline", "xline", None),
        P("inline", "xline", None),
        P(),
        P("inline", "xline", None),
        P("inline", "xline", None),
        P(("inline", "xline")),
        P(("inline", "xline"), None),
        P(("inline", "xline")),
        P(("inline", "xline")),
    )
    out_specs = (P("inline", "xline", None), P("inline", "xline", None))
    return jax.shard_map(body, mesh=mesh, in_specs=in_specs, out_specs=out_specs, check_vma=False)
```
